512 devices in a mesh: dp: 64 (over x, z), cent: 8 (over y, core).
Axes of the slice: x: 4, y: 4, z: 16, core: 2. Of those that a mesh axis runs over, the one named last changes fastest.
Arguments:
- embeddings: bfloat16 [131072, 768], P('dp'), may hold values from -8 to 8
- coarse_ids: int32 [131072, 16], P('dp'), may hold values from 0 to 511, as said below
- centroids: float32 [8192, 768], P(('dp', 'cent')), may hold values from -4 to 4
- coarse_of: int32 [8192], replicated, may hold values from 0 to 511, as said below
Outputs:
- new_centroids: float32 [8192, 768], P(('dp', 'cent'))
The draws below stay inside these ranges and needn't reach their ends.
Inputs may be any that keep to these rules, and one draw needn't show every extreme that they name: `coarse_of`: each coarse cluster holds exactly 16 centroids. `coarse_ids`: the 16 entries of a row are distinct and increase along the row; every coarse cluster is named by some row.
All inputs are finite; a program needn't handle non-finite values.
Results may differ from the reference program's by a relative error of at most 0.003.
Values may be sent and summed in bfloat16 or wider, within the bound.
No kernel may reach another device: no remote copies, remote signals or barrier semaphores. Data moves between devices by JAX's collectives and lax.ppermute only.
A program may use at most 64 MiB of HBM per device.

```python
import math
import jax
import jax.numpy as jnp
from jax import lax

D = 768
ROWS_DEV = 2048
K_SH = 16
PER_COARSE = 16
PICKS = 16
SWEEPS = 3
ROWS = 131072
K = 8192
N_DP = 64
N_CENT = 8


def centroid_order(key):
    return jax.random.permutation(jax.random.fold_in(key, 101), K).astype(jnp.int32)


def centroid_values(key):
    values = jax.random.normal(jax.random.fold_in(key, 103), (K, D), jnp.float32)
    return jnp.clip(values, -4.0, 4.0)


def row_picks(key):
    clusters = K // PER_COARSE
    row_count = ROWS
    cluster_perm = jax.random.permutation(jax.random.fold_in(key, 104), clusters).astype(jnp.int32)
    compelled_choice = cluster_perm[jnp.arange(row_count, dtype=jnp.int32) % clusters]
    cluster_rank = jax.random.permutation(jax.random.fold_in(key, 105), clusters).astype(jnp.int32)
    demand_level = 16384 // (cluster_rank + 8)
    noisy_ratings = jax.random.randint(jax.random.fold_in(key, 106), (row_count, clusters), 0, 4096, jnp.int32)
    column_labels = jnp.arange(clusters, dtype=jnp.int32)
    reward_boost = 8192 * (column_labels[None, :] == compelled_choice[:, None]).astype(jnp.int32)
    match_ratings = noisy_ratings + demand_level[None, :] + reward_boost
    distinct = match_ratings * clusters + column_labels[None, :]
    unused, chosen = lax.top_k(distinct, PICKS)
    return (jnp.sort(chosen.astype(jnp.int32), axis=1), compelled_choice)


def draw_coarse_of(key, part):
    order = centroid_order(key)
    return (order % (K // PER_COARSE)).astype(jnp.int32)


def draw_coarse_ids(key, part):
    chosen, compelled_choice = row_picks(key)
    return chosen


def draw_centroids(key, part):
    values = centroid_values(key)
    return values


def draw_embeddings(key, part):
    order = centroid_order(key)
    chosen, compelled_choice = row_picks(key)
    values = centroid_values(key)
    key = jax.random.fold_in(key, 17)
    clusters = K // PER_COARSE
    row_count = ROWS
    keys = jax.random.split(key, 4)
    favoured = jax.random.randint(keys[0], (row_count,), 0, 2, jnp.int32)
    member = jax.random.randint(keys[1], (row_count,), 0, PER_COARSE, jnp.int32) * favoured
    assignment_grid = jnp.argsort(order, stable=True).astype(jnp.int32)
    preferred = assignment_grid[compelled_choice + member * clusters]
    strength = jnp.exp(jax.random.uniform(keys[2], (row_count,), jnp.float32, jnp.log(0.15), jnp.log(2.5)))
    background = jax.random.normal(keys[3], (row_count, D), jnp.float32)
    combined = strength[:, None] * values[preferred] + background
    return jnp.clip(combined, -8.0, 8.0).astype(jnp.bfloat16)


def setup_inputs(seed: int = 0) -> dict:
    key_list = jax.random.split(jax.random.key(seed), 5)
    return {
        "embeddings": draw_embeddings(jax.random.fold_in(key_list[4], 71), 0),
        "coarse_ids": draw_coarse_ids(jax.random.fold_in(key_list[4], 71), 0),
        "centroids": draw_centroids(jax.random.fold_in(key_list[4], 71), 0),
        "coarse_of": draw_coarse_of(jax.random.fold_in(key_list[4], 71), 0),
    }


entropic_smoothing = 0.03

def unit_rows(values):
    values = values.astype(jnp.float32)
    return values * lax.rsqrt(lax.optimization_barrier(jnp.sum(values * values, axis=-1, keepdims=True)) + 1e-06)

def reference(embeddings, coarse_ids, centroids, coarse_of):
    total_rows = ROWS_DEV * N_DP
    centroid_count = K_SH * N_DP * N_CENT
    desired_load = total_rows / centroid_count
    unit_x = unit_rows(embeddings).astype(jnp.bfloat16)
    unit_c = unit_rows(centroids).astype(jnp.bfloat16)
    cluster_population = jnp.argsort(coarse_of, stable=True).astype(jnp.int32).reshape(centroid_count // PER_COARSE, PER_COARSE)
    picked = cluster_population[coarse_ids].astype(jnp.int32)
    block_count = total_rows // 64

    def tile_similarity_matrix(pair):
        point_tile, label_tile = pair
        gathered = unit_c[label_tile].astype(jnp.float32)
        pairwise_dots = jnp.einsum('bd,bpkd->bpk', point_tile.astype(jnp.float32), gathered)
        return jnp.exp(pairwise_dots / entropic_smoothing)
    similarity_exponential = lax.map(tile_similarity_matrix, (unit_x.reshape(block_count, 64, D), picked.reshape(block_count, 64, PICKS, PER_COARSE)))
    similarity_exponential = similarity_exponential.reshape(total_rows, PICKS, PER_COARSE)
    flat_ids = picked.reshape(-1)
    row_scaling = 1.0 / lax.optimization_barrier(jnp.sum(similarity_exponential, axis=(1, 2)))
    for sweep in range(SWEEPS):
        column = jax.ops.segment_sum((similarity_exponential * row_scaling[:, None, None]).reshape(-1), flat_ids, num_segments=centroid_count)
        col_factor = desired_load / column
        row_scaling = 1.0 / lax.optimization_barrier(jnp.sum(similarity_exponential * col_factor[picked], axis=(1, 2)))
    weighted = similarity_exponential * row_scaling[:, None, None]
    mass = jax.ops.segment_sum(weighted.reshape(-1), flat_ids, num_segments=centroid_count)
    rounded = weighted.astype(jnp.bfloat16)
    block = math.gcd(total_rows, 1024)
    steps_count = total_rows // block

    def add_block(total, pair):
        point_tile, w_block, label_tile = pair
        dense = jnp.zeros((block, centroid_count), jnp.bfloat16).at[jnp.arange(block)[:, None, None], label_tile].set(w_block)
        part_sum = lax.dot_general(dense, point_tile, (((0,), (0,)), ((), ())), preferred_element_type=jnp.float32)
        return (total + part_sum, None)
    numerator, unused = lax.scan(add_block, jnp.zeros((centroid_count, D), jnp.float32), (embeddings.reshape(steps_count, block, D), rounded.reshape(steps_count, block, PICKS, PER_COARSE), picked.reshape(steps_count, block, PICKS, PER_COARSE)))
    return (numerator + centroids) / (mass + 1.0)[:, None]
```

```python
import jax
import jax.numpy as jnp
from jax import lax
from jax.sharding import Mesh
from jax.sharding import PartitionSpec as P

SWEEPS = 3


entropic_smoothing = 0.03


def unit_rows(values):
    values = values.astype(jnp.float32)
    return values * lax.rsqrt(jnp.sum(values * values, axis=-1, keepdims=True) + 1e-06)


def exchange(blocks, axes):
    return lax.all_to_all(blocks, axes, 0, 0)


def spread(block, axes):
    copies = jnp.broadcast_to(block[None], (lax.axis_size(axes),) + block.shape)
    return exchange(copies, axes)


def row_scale(similarity_exponential, col_factor):
    part = jnp.sum(similarity_exponential * col_factor[None, :], axis=1)
    totals = jnp.sum(spread(part.reshape(-1, 128), ("y", "core")), axis=0)
    return 1.0 / totals.reshape(-1)


def column_scale(similarity_exponential, row_scaling, desired_load):
    part = jnp.sum(similarity_exponential * row_scaling[:, None], axis=0).reshape(-1, 128)
    part = jnp.sum(spread(part, "x"), axis=0)
    part = jnp.sum(spread(part, "z"), axis=0)
    return desired_load / part.reshape(-1)


def per_device(embeddings, coarse_ids, centroids, coarse_of):
    row_count = embeddings.shape[0]
    local_count, width = centroids.shape
    x_size, z_size = lax.axis_size("x"), lax.axis_size("z")
    dp_size = x_size * z_size
    cent_size = lax.axis_size(("y", "core"))
    desired_load = row_count / (local_count * cent_size)
    unit_x = unit_rows(embeddings).astype(jnp.bfloat16)
    unit_c = unit_rows(centroids).astype(jnp.bfloat16)
    layout_table = coarse_of.reshape(dp_size, cent_size, local_count)
    group_ids = lax.dynamic_slice_in_dim(
        layout_table, lax.axis_index(("y", "core")), 1, 1
    ).reshape(dp_size * local_count)
    along_z = spread(unit_c, "z")
    group_centroids = spread(along_z, "x").reshape(dp_size * local_count, width)
    pairwise_dots = lax.dot_general(
        unit_x, group_centroids, (((1,), (1,)), ((), ())), preferred_element_type=jnp.float32
    )
    assigned_points = jnp.any(coarse_ids[:, :, None] == group_ids[None, None, :], axis=1)
    similarity_exponential = jnp.where(
        assigned_points, jnp.exp(pairwise_dots / entropic_smoothing), 0.0
    )
    row_scaling = row_scale(
        similarity_exponential, jnp.ones((similarity_exponential.shape[1],), jnp.float32)
    )
    for sweep in range(SWEEPS):
        col_factor = column_scale(similarity_exponential, row_scaling, desired_load)
        row_scaling = row_scale(similarity_exponential, col_factor)
    weighted = similarity_exponential * row_scaling[:, None]
    col_mass = jnp.sum(weighted, axis=0)
    numerator = lax.dot_general(
        weighted.astype(jnp.bfloat16),
        embeddings,
        (((0,), (0,)), ((), ())),
        preferred_element_type=jnp.float32,
    )
    sums = jnp.concatenate(
        [numerator, jnp.broadcast_to(col_mass[:, None], (col_mass.shape[0], 128))], axis=1
    )
    sums = sums.astype(jnp.bfloat16).reshape(x_size, z_size, local_count, width + 128)
    sums = jnp.sum(exchange(sums, "x").astype(jnp.float32), axis=0)
    sums = jnp.sum(exchange(sums.astype(jnp.bfloat16), "z").astype(jnp.float32), axis=0)
    numer_own, mass_own = sums[:, :width], sums[:, width]
    return (numer_own + centroids) / (mass_own + 1.0)[:, None]


def solution(mesh):
    fine = Mesh(mesh.devices.reshape(4, 16, 4, 2), ("x", "z", "y", "core"))
    return jax.shard_map(
        per_device,
        mesh=fine,
        in_specs=(
            P(("x", "z"), None),
            P(("x", "z"), None),
            P(("x", "z", "y", "core"), None),
            P(),
        ),
        out_specs=P(("x", "z", "y", "core"), None),
        check_vma=False,
    )
```

```python
import functools
import math

import jax
import jax.numpy as jnp
from jax import lax
from jax.experimental import pallas as pl
from jax.experimental.pallas import tpu as pltpu
from jax.sharding import Mesh
from jax.sharding import PartitionSpec as P

SWEEPS = 3
CLUSTERS = 512
LANES = 128
TILE = 256


entropic_smoothing = 0.03
MIB = 1 << 20
f32, bf16 = jnp.float32, jnp.bfloat16


def unit_rows(values):
    values = values.astype(f32)
    return values * lax.rsqrt(jnp.sum(values * values, axis=-1, keepdims=True) + 1e-06)


def exchange(blocks, axes):
    return lax.all_to_all(blocks, axes, 0, 0)


def spread(block, axes):
    copies = jnp.broadcast_to(block[None], (lax.axis_size(axes),) + block.shape)
    return exchange(copies, axes)


def as_row(tiles):
    return jnp.concatenate([tiles[q : q + 1] for q in range(tiles.shape[0])], axis=1)


def as_tiles(row):
    count = row.shape[1] // LANES
    return jnp.concatenate([row[:, q * LANES : (q + 1) * LANES] for q in range(count)], axis=0)


def two_terms(row):
    wide = jnp.broadcast_to(row, (16, row.shape[1]))
    high = wide.astype(bf16).astype(f32)
    which = lax.broadcasted_iota(jnp.int32, wide.shape, 0)
    rest = jnp.where(which == 1, wide - high, 0.0)
    return jnp.where(which == 0, high, rest).astype(bf16)


def prepare_kernel(x_ref, ids_ref, group_ref, unit_ref, match_ref, hot_ref):
    @pl.when(pl.program_id(0) == 0)
    def _():
        cluster = lax.broadcasted_iota(jnp.int32, hot_ref.shape, 0)
        hot_ref[...] = jnp.where(cluster == group_ref[...], 1.0, 0.0).astype(bf16)

    unit_ref[...] = unit_rows(x_ref[...]).astype(bf16)
    ids = ids_ref[...]
    cluster = lax.broadcasted_iota(jnp.int32, (ids.shape[0], CLUSTERS), 1)
    picked = jnp.zeros(cluster.shape, f32)
    for p in range(ids.shape[1]):
        picked = jnp.where(ids[:, p : p + 1] == cluster, 1.0, picked)
    match_ref[...] = jnp.dot(picked.astype(bf16), hot_ref[...], preferred_element_type=f32).astype(bf16)


def similarity_kernel(unit_ref, cent_ref, match_ref, sim_ref, total_ref):
    ones = jnp.ones((total_ref.shape[0], sim_ref.shape[1]), bf16)
    scale = math.log2(math.e) / entropic_smoothing
    for b in range(unit_ref.shape[0] // TILE):
        rows = pl.ds(b * TILE, TILE)
        dots = lax.dot_general(
            unit_ref[rows, :], cent_ref[...], (((1,), (1,)), ((), ())), preferred_element_type=f32
        )
        sim = (jnp.exp2(dots * scale) * match_ref[rows, :].astype(f32)).astype(bf16)
        sim_ref[rows, :] = sim
        totals = lax.dot_general(ones, sim, (((1,), (1,)), ((), ())), preferred_element_type=f32)
        for q in range(TILE // LANES):
            total_ref[:, b * (TILE // LANES) + q, :] = totals[:, q * LANES : (q + 1) * LANES]


def column_kernel(parts_ref, sim_ref, out_ref):
    factor = 1.0 / jnp.sum(parts_ref[...], axis=0)
    lhs = two_terms(as_row(factor))
    sums = jnp.dot(lhs, sim_ref[...], preferred_element_type=f32)
    out_ref[...] = jnp.broadcast_to(as_tiles(jnp.sum(sums, axis=0, keepdims=True))[None], out_ref.shape)


def row_kernel(desired_load, parts_ref, sim_ref, out_ref):
    factor = desired_load / jnp.sum(parts_ref[...], axis=0)
    lhs = two_terms(as_row(factor))
    sums = lax.dot_general(lhs, sim_ref[...], (((1,), (1,)), ((), ())), preferred_element_type=f32)
    out_ref[...] = jnp.broadcast_to(as_tiles(jnp.sum(sums, axis=0, keepdims=True))[None], out_ref.shape)


def down(row):
    return jnp.transpose(jnp.broadcast_to(row, (LANES, LANES)))


def numerator_kernel(parts_ref, sim_ref, x_ref, out_ref, weight_ref):
    factor = 1.0 / jnp.sum(parts_ref[...], axis=0)
    lhs = two_terms(as_row(factor))
    mass = jnp.sum(jnp.dot(lhs, sim_ref[...], preferred_element_type=f32), axis=0, keepdims=True)
    columns = sim_ref.shape[1]
    for q in range(sim_ref.shape[0] // LANES):
        rows = pl.ds(q * LANES, LANES)
        scale = jnp.concatenate([down(factor[q : q + 1])] * (columns // LANES), axis=1)
        weight_ref[rows, :] = (sim_ref[rows, :].astype(f32) * scale).astype(bf16)
    width = x_ref.shape[1]
    for b in range(columns // TILE):
        rows = pl.ds(b * TILE, TILE)
        out_ref[rows, :width] = lax.dot_general(
            weight_ref[:, rows], x_ref[...], (((0,), (0,)), ((), ())), preferred_element_type=f32
        ).astype(bf16)
    for q in range(columns // LANES):
        out_ref[pl.ds(q * LANES, LANES), width:] = down(mass[:, q * LANES : (q + 1) * LANES]).astype(bf16)


def call(kernel, name, operands, outs, mib, flops, scratch=()):
    moved = sum(math.prod(o.shape) * o.dtype.itemsize for o in (*operands, *outs))
    vmem = pl.BlockSpec(memory_space=pltpu.VMEM)
    single = len(outs) == 1
    return pl.pallas_call(
        kernel,
        name=name,
        out_shape=outs[0] if single else outs,
        in_specs=[vmem] * len(operands),
        out_specs=vmem if single else [vmem] * len(outs),
        scratch_shapes=scratch,
        compiler_params=pltpu.CompilerParams(vmem_limit_bytes=mib * MIB),
        cost_estimate=pl.CostEstimate(flops=flops, bytes_accessed=moved, transcendentals=0),
    )(*operands)


def prepare(embeddings, coarse_ids, group_ids):
    rows, width = embeddings.shape
    columns = group_ids.shape[1]
    return pl.pallas_call(
        prepare_kernel,
        name="prepare",
        grid=(rows // TILE,),
        in_specs=[
            pl.BlockSpec((TILE, width), lambda i: (i, 0)),
            pl.BlockSpec((TILE, coarse_ids.shape[1]), lambda i: (i, 0)),
            pl.BlockSpec((1, columns), lambda i: (0, 0)),
        ],
        out_specs=[
            pl.BlockSpec((TILE, width), lambda i: (i, 0)),
            pl.BlockSpec((TILE, columns), lambda i: (i, 0)),
        ],
        out_shape=[
            jax.ShapeDtypeStruct((rows, width), bf16),
            jax.ShapeDtypeStruct((rows, columns), bf16),
        ],
        scratch_shapes=[pltpu.VMEM((CLUSTERS, columns), bf16)],
        compiler_params=pltpu.CompilerParams(vmem_limit_bytes=16 * MIB),
        cost_estimate=pl.CostEstimate(
            flops=8 * rows * CLUSTERS * columns, bytes_accessed=32 * rows * width, transcendentals=0
        ),
    )(embeddings, coarse_ids, group_ids)


def per_device(embeddings, coarse_ids, centroids, coarse_of):
    row_count, width = embeddings.shape
    local_count = centroids.shape[0]
    x_size, z_size = lax.axis_size("x"), lax.axis_size("z")
    dp_size = x_size * z_size
    cent_size = lax.axis_size(("y", "core"))
    columns = dp_size * local_count
    desired_load = row_count / (local_count * cent_size)
    unit_c = unit_rows(centroids).astype(bf16)
    layout_table = coarse_of.reshape(dp_size, cent_size, local_count)
    group_ids = lax.dynamic_slice_in_dim(
        layout_table, lax.axis_index(("y", "core")), 1, 1
    ).reshape(1, columns)
    unit_x, matched = prepare(embeddings, coarse_ids, group_ids)
    along_z = spread(unit_c, "z")
    group_centroids = spread(along_z, "x").reshape(columns, width)

    product = 2 * row_count * columns
    row_parts = jax.ShapeDtypeStruct((cent_size, row_count // LANES, LANES), f32)
    column_parts = jax.ShapeDtypeStruct((x_size, columns // LANES, LANES), f32)
    similarity, parts = call(
        similarity_kernel,
        "similarity",
        (unit_x, group_centroids, matched),
        (jax.ShapeDtypeStruct((row_count, columns), bf16), row_parts),
        16,
        product * width,
    )
    parts = exchange(parts, ("y", "core"))
    for sweep in range(SWEEPS):
        parts = call(column_kernel, "columns", (parts, similarity), (column_parts,), 8, product * 16)
        parts = jnp.sum(exchange(parts, "x"), axis=0)
        parts = spread(parts, "z")
        parts = call(
            functools.partial(row_kernel, desired_load),
            "rows",
            (parts, similarity),
            (row_parts,),
            8,
            product * 16,
        )
        parts = exchange(parts, ("y", "core"))
    sums = call(
        numerator_kernel,
        "numerator",
        (parts, similarity, embeddings),
        (jax.ShapeDtypeStruct((columns, width + LANES), bf16),),
        16,
        product * width,
        scratch=[pltpu.VMEM((row_count, columns), bf16)],
    )
    sums = sums.reshape(x_size, z_size, local_count, width + LANES)
    sums = jnp.sum(exchange(sums, "x").astype(f32), axis=0)
    sums = jnp.sum(exchange(sums.astype(bf16), "z").astype(f32), axis=0)
    numer_own, mass_own = sums[:, :width], sums[:, width]
    return (numer_own + centroids) / (mass_own + 1.0)[:, None]


def solution(mesh):
    fine = Mesh(mesh.devices.reshape(4, 16, 4, 2), ("x", "z", "y", "core"))
    return jax.shard_map(
        per_device,
        mesh=fine,
        in_specs=(
            P(("x", "z"), None),
            P(("x", "z"), None),
            P(("x", "z", "y", "core"), None),
            P(),
        ),
        out_specs=P(("x", "z", "y", "core"), None),
        check_vma=False,
    )
```

```python
import functools
import math

import jax
import jax.numpy as jnp
from jax import lax
from jax.experimental import pallas as pl
from jax.experimental.pallas import tpu as pltpu
from jax.sharding import Mesh
from jax.sharding import PartitionSpec as P

SWEEPS = 3
CLUSTERS = 512
LANES = 128
TILE = 256


entropic_smoothing = 0.03
MIB = 1 << 20
f32, bf16 = jnp.float32, jnp.bfloat16


def unit_rows(values):
    values = values.astype(f32)
    return values * lax.rsqrt(jnp.sum(values * values, axis=-1, keepdims=True) + 1e-06)


def exchange(blocks, axes):
    return lax.all_to_all(blocks, axes, 0, 0)


def as_row(tiles):
    return jnp.concatenate([tiles[q : q + 1] for q in range(tiles.shape[0])], axis=1)


def as_tiles(row):
    count = row.shape[1] // LANES
    return jnp.concatenate([row[:, q * LANES : (q + 1) * LANES] for q in range(count)], axis=0)


def two_terms(row):
    wide = jnp.broadcast_to(row, (16, row.shape[1]))
    high = wide.astype(bf16).astype(f32)
    which = lax.broadcasted_iota(jnp.int32, wide.shape, 0)
    rest = jnp.where(which == 1, wide - high, 0.0)
    return jnp.where(which == 0, high, rest).astype(bf16)


def prepare_kernel(x_ref, ids_ref, group_ref, unit_ref, match_ref, hot_ref):
    @pl.when(pl.program_id(0) == 0)
    def _():
        cluster = lax.broadcasted_iota(jnp.int32, hot_ref.shape, 0)
        hot_ref[...] = jnp.where(cluster == group_ref[...], 1.0, 0.0).astype(bf16)

    unit_ref[...] = unit_rows(x_ref[...]).astype(bf16)
    ids = ids_ref[...]
    cluster = lax.broadcasted_iota(jnp.int32, (ids.shape[0], CLUSTERS), 1)
    picked = jnp.zeros(cluster.shape, f32)
    for p in range(ids.shape[1]):
        picked = jnp.where(ids[:, p : p + 1] == cluster, 1.0, picked)
    match_ref[...] = jnp.dot(picked.astype(bf16), hot_ref[...], preferred_element_type=f32).astype(bf16)


def unit_copies_kernel(cent_ref, out_ref):
    out_ref[...] = jnp.broadcast_to(unit_rows(cent_ref[...]).astype(bf16)[None], out_ref.shape)


def copies_kernel(block_ref, out_ref):
    for i in range(out_ref.shape[0]):
        out_ref[i] = block_ref[...]


def sum_copies_kernel(parts_ref, out_ref):
    out_ref[...] = jnp.broadcast_to(jnp.sum(parts_ref[...], axis=0)[None], out_ref.shape)


def similarity_kernel(unit_any, cent_ref, match_any, sim_ref, total_ref, unit_ref, match_ref, sems):
    copies = []
    for b in range(unit_ref.shape[0] // TILE):
        rows = pl.ds(b * TILE, TILE)
        pair = (
            pltpu.make_async_copy(unit_any.at[rows], unit_ref.at[rows], sems.at[0, b]),
            pltpu.make_async_copy(match_any.at[rows], match_ref.at[rows], sems.at[1, b]),
        )
        for copy in pair:
            copy.start()
        copies.append(pair)
    ones = jnp.ones((total_ref.shape[0], sim_ref.shape[1]), bf16)
    scale = math.log2(math.e) / entropic_smoothing
    for b, pair in enumerate(copies):
        rows = pl.ds(b * TILE, TILE)
        for copy in pair:
            copy.wait()
        dots = lax.dot_general(
            unit_ref[rows, :], cent_ref[...], (((1,), (1,)), ((), ())), preferred_element_type=f32
        )
        sim = (jnp.exp2(dots * scale) * match_ref[rows, :].astype(f32)).astype(bf16)
        sim_ref[rows, :] = sim
        totals = lax.dot_general(ones, sim, (((1,), (1,)), ((), ())), preferred_element_type=f32)
        for q in range(TILE // LANES):
            total_ref[:, b * (TILE // LANES) + q, :] = totals[:, q * LANES : (q + 1) * LANES]


def column_kernel(parts_ref, sim_ref, out_ref):
    factor = 1.0 / jnp.sum(parts_ref[...], axis=0)
    lhs = two_terms(as_row(factor))
    sums = jnp.dot(lhs, sim_ref[...], preferred_element_type=f32)
    out_ref[...] = jnp.broadcast_to(as_tiles(jnp.sum(sums, axis=0, keepdims=True))[None], out_ref.shape)


def row_kernel(desired_load, parts_ref, sim_ref, out_ref):
    factor = desired_load / jnp.sum(parts_ref[...], axis=0)
    lhs = two_terms(as_row(factor))
    sums = lax.dot_general(lhs, sim_ref[...], (((1,), (1,)), ((), ())), preferred_element_type=f32)
    out_ref[...] = jnp.broadcast_to(as_tiles(jnp.sum(sums, axis=0, keepdims=True))[None], out_ref.shape)


def down(row):
    return jnp.transpose(jnp.broadcast_to(row, (LANES, LANES)))


def numerator_kernel(count, parts_ref, sim_ref, x_ref, out_ref, weight_ref):
    factor = 1.0 / jnp.sum(parts_ref[...], axis=0)
    lhs = two_terms(as_row(factor))
    mass = jnp.sum(jnp.dot(lhs, sim_ref[...], preferred_element_type=f32), axis=0, keepdims=True)
    columns = sim_ref.shape[1]
    for q in range(sim_ref.shape[0] // LANES):
        rows = pl.ds(q * LANES, LANES)
        scale = jnp.concatenate([down(factor[q : q + 1])] * (columns // LANES), axis=1)
        weight_ref[rows, :] = (sim_ref[rows, :].astype(f32) * scale).astype(bf16)
    chunks = x_ref.shape[1] // LANES
    held = columns // out_ref.shape[0]
    base = held * chunks
    for i in range(out_ref.shape[0]):
        sums = lax.dot_general(
            weight_ref[:, pl.ds(i * held, held)],
            x_ref[...],
            (((0,), (0,)), ((), ())),
            preferred_element_type=f32,
        ).astype(bf16)
        for z in range(held // count):
            for c in range(chunks):
                out_ref[i, pl.ds((z * chunks + c) * count, count), :] = sums[
                    z * count : (z + 1) * count, c * LANES : (c + 1) * LANES
                ]
        own = as_tiles(mass[:, i * held : (i + 1) * held])
        rest = jnp.zeros((out_ref.shape[1] - base - own.shape[0], LANES), f32)
        out_ref[i, pl.ds(base, out_ref.shape[1] - base), :] = jnp.concatenate([own, rest], axis=0).astype(bf16)


def hand_on_kernel(count, parts_ref, out_ref):
    total = jnp.sum(parts_ref[...].astype(f32), axis=0)
    chunk_rows = out_ref.shape[1] - 16
    base = chunk_rows * out_ref.shape[0]
    for z in range(out_ref.shape[0]):
        out_ref[z, pl.ds(0, chunk_rows), :] = total[z * chunk_rows : (z + 1) * chunk_rows].astype(bf16)
        at = z * count % LANES
        row = total[base + z * count // LANES : base + z * count // LANES + 1]
        row = jnp.concatenate([row[:, at:], row[:, :at]], axis=1) if at else row
        out_ref[z, pl.ds(chunk_rows, 16), :] = jnp.broadcast_to(row, (16, LANES)).astype(bf16)


def update_kernel(parts_ref, cent_ref, out_ref):
    total = jnp.sum(parts_ref[...].astype(f32), axis=0)
    count, width = out_ref.shape
    chunk_rows = width // LANES * count
    scale = 1.0 / (down(total[chunk_rows : chunk_rows + 1])[:count] + 1.0)
    for c in range(width // LANES):
        lanes = pl.ds(c * LANES, LANES)
        out_ref[:, lanes] = (total[c * count : (c + 1) * count] + cent_ref[:, lanes]) * scale


def call(kernel, name, operands, outs, mib, flops, scratch=(), anywhere=()):
    moved = sum(math.prod(o.shape) * o.dtype.itemsize for o in (*operands, *outs))
    vmem, place = pl.BlockSpec(memory_space=pltpu.VMEM), pl.BlockSpec(memory_space=pl.ANY)
    single = len(outs) == 1
    return pl.pallas_call(
        kernel,
        name=name,
        out_shape=outs[0] if single else outs,
        in_specs=[place if i in anywhere else vmem for i in range(len(operands))],
        out_specs=vmem if single else [vmem] * len(outs),
        scratch_shapes=scratch,
        compiler_params=pltpu.CompilerParams(vmem_limit_bytes=mib * MIB),
        cost_estimate=pl.CostEstimate(flops=flops, bytes_accessed=moved, transcendentals=0),
    )(*operands)


def prepare(embeddings, coarse_ids, group_ids):
    rows, width = embeddings.shape
    columns = group_ids.shape[1]
    return pl.pallas_call(
        prepare_kernel,
        name="prepare",
        grid=(rows // TILE,),
        in_specs=[
            pl.BlockSpec((TILE, width), lambda i: (i, 0)),
            pl.BlockSpec((TILE, coarse_ids.shape[1]), lambda i: (i, 0)),
            pl.BlockSpec((1, columns), lambda i: (0, 0)),
        ],
        out_specs=[
            pl.BlockSpec((TILE, width), lambda i: (i, 0)),
            pl.BlockSpec((TILE, columns), lambda i: (i, 0)),
        ],
        out_shape=[
            jax.ShapeDtypeStruct((rows, width), bf16),
            jax.ShapeDtypeStruct((rows, columns), bf16),
        ],
        scratch_shapes=[pltpu.VMEM((CLUSTERS, columns), bf16)],
        compiler_params=pltpu.CompilerParams(vmem_limit_bytes=16 * MIB),
        cost_estimate=pl.CostEstimate(
            flops=8 * rows * CLUSTERS * columns, bytes_accessed=32 * rows * width, transcendentals=0
        ),
    )(embeddings, coarse_ids, group_ids)


def per_device(embeddings, coarse_ids, centroids, coarse_of):
    row_count, width = embeddings.shape
    local_count = centroids.shape[0]
    x_size, z_size = lax.axis_size("x"), lax.axis_size("z")
    dp_size = x_size * z_size
    cent_size = lax.axis_size(("y", "core"))
    columns = dp_size * local_count
    desired_load = row_count / (local_count * cent_size)
    layout_table = coarse_of.reshape(dp_size, cent_size, local_count)
    group_ids = lax.dynamic_slice_in_dim(
        layout_table, lax.axis_index(("y", "core")), 1, 1
    ).reshape(1, columns)
    unit_x, matched = prepare(embeddings, coarse_ids, group_ids)

    array = jax.ShapeDtypeStruct
    copies = call(
        unit_copies_kernel, "units", (centroids,), (array((z_size, local_count, width), bf16),), 4, 0
    )
    along_z = exchange(copies, "z")
    copies = call(copies_kernel, "copies", (along_z,), (array((x_size,) + along_z.shape, bf16),), 4, 0)
    group_centroids = exchange(copies, "x").reshape(columns, width)

    product = 2 * row_count * columns
    row_parts = array((cent_size, row_count // LANES, LANES), f32)
    column_parts = array((x_size, columns // LANES, LANES), f32)
    column_sums = array((z_size, columns // LANES, LANES), f32)
    similarity, parts = call(
        similarity_kernel,
        "similarity",
        (unit_x, group_centroids, matched),
        (array((row_count, columns), bf16), row_parts),
        20,
        product * width,
        scratch=[
            pltpu.VMEM((row_count, width), bf16),
            pltpu.VMEM((row_count, columns), bf16),
            pltpu.SemaphoreType.DMA((2, row_count // TILE)),
        ],
        anywhere=(0, 2),
    )
    parts = exchange(parts, ("y", "core"))
    for sweep in range(SWEEPS):
        parts = call(column_kernel, "columns", (parts, similarity), (column_parts,), 8, product * 16)
        parts = call(sum_copies_kernel, "across", (exchange(parts, "x"),), (column_sums,), 2, 0)
        parts = call(
            functools.partial(row_kernel, desired_load),
            "rows",
            (exchange(parts, "z"), similarity),
            (row_parts,),
            8,
            product * 16,
        )
        parts = exchange(parts, ("y", "core"))
    chunk_rows = width // LANES * local_count
    sums = call(
        functools.partial(numerator_kernel, local_count),
        "numerator",
        (parts, similarity, embeddings),
        (array((x_size, z_size * chunk_rows + 16, LANES), bf16),),
        16,
        product * width,
        scratch=[pltpu.VMEM((row_count, columns), bf16)],
    )
    sums = call(
        functools.partial(hand_on_kernel, local_count),
        "hand_on",
        (exchange(sums, "x"),),
        (array((z_size, chunk_rows + 16, LANES), bf16),),
        8,
        0,
    )
    return call(
        update_kernel,
        "update",
        (exchange(sums, "z"), centroids),
        (array(centroids.shape, f32),),
        4,
        0,
    )


def solution(mesh):
    fine = Mesh(mesh.devices.reshape(4, 16, 4, 2), ("x", "z", "y", "core"))
    return jax.shard_map(
        per_device,
        mesh=fine,
        in_specs=(
            P(("x", "z"), None),
            P(("x", "z"), None),
            P(("x", "z", "y", "core"), None),
            P(),
        ),
        out_specs=P(("x", "z", "y", "core"), None),
        check_vma=False,
    )
```

```python
import functools
import math

import jax
import jax.numpy as jnp
from jax import lax
from jax.experimental import pallas as pl
from jax.experimental.pallas import tpu as pltpu
from jax.sharding import Mesh
from jax.sharding import PartitionSpec as P

SWEEPS = 3
CLUSTERS = 512
LANES = 128
TILE = 256


entropic_smoothing = 0.03
MIB = 1 << 20
f32, bf16 = jnp.float32, jnp.bfloat16


def unit_rows(values):
    values = values.astype(f32)
    return values * lax.rsqrt(jnp.sum(values * values, axis=-1, keepdims=True) + 1e-06)


def exchange(blocks, axes):
    return lax.all_to_all(blocks, axes, 0, 0)


def as_row(tiles):
    return jnp.concatenate([tiles[q : q + 1] for q in range(tiles.shape[0])], axis=1)


def as_tiles(row):
    count = row.shape[1] // LANES
    return jnp.concatenate([row[:, q * LANES : (q + 1) * LANES] for q in range(count)], axis=0)


def two_terms(row):
    wide = jnp.broadcast_to(row, (16, row.shape[1]))
    high = wide.astype(bf16).astype(f32)
    which = lax.broadcasted_iota(jnp.int32, wide.shape, 0)
    rest = jnp.where(which == 1, wide - high, 0.0)
    return jnp.where(which == 0, high, rest).astype(bf16)


def prepare_kernel(x_ref, ids_ref, group_ref, unit_hbm, match_hbm, unit_ref, match_ref, hot_ref, sems):
    cluster = lax.broadcasted_iota(jnp.int32, hot_ref.shape, 0)
    hot_ref[...] = jnp.where(cluster == group_ref[...], 1.0, 0.0).astype(bf16)

    def copies(b):
        rows = pl.ds(b * TILE, TILE)
        return (
            pltpu.make_async_copy(unit_ref.at[rows], unit_hbm.at[rows], sems.at[0, b]),
            pltpu.make_async_copy(match_ref.at[rows], match_hbm.at[rows], sems.at[1, b]),
        )

    def block(b):
        rows = pl.ds(b * TILE, TILE)
        unit_ref[rows, :] = unit_rows(x_ref[rows, :]).astype(bf16)
        ids = ids_ref[rows, :]
        cluster = lax.broadcasted_iota(jnp.int32, (TILE, CLUSTERS), 1)
        picked = jnp.zeros(cluster.shape, f32)
        for p in range(ids.shape[1]):
            picked = jnp.where(ids[:, p : p + 1] == cluster, 1.0, picked)
        matched = jnp.dot(picked.astype(bf16), hot_ref[...], preferred_element_type=f32)
        match_ref[rows, :] = matched.astype(bf16)

    count = x_ref.shape[0] // TILE
    for b in range(count):
        block(b)
        for copy in copies(b):
            copy.start()
    for b in range(count):
        for copy in copies(b):
            copy.wait()


def unit_copies_kernel(cent_ref, out_ref):
    out_ref[...] = jnp.broadcast_to(unit_rows(cent_ref[...]).astype(bf16)[None], out_ref.shape)


def copies_kernel(block_ref, out_ref):
    for i in range(out_ref.shape[0]):
        out_ref[i] = block_ref[...]


def sum_copies_kernel(parts_ref, out_ref):
    out_ref[...] = jnp.broadcast_to(jnp.sum(parts_ref[...], axis=0)[None], out_ref.shape)


def similarity_kernel(unit_hbm, cent_ref, match_hbm, sim_ref, total_ref, unit_ref, match_ref, sems):
    copies = []
    for b in range(unit_ref.shape[0] // TILE):
        rows = pl.ds(b * TILE, TILE)
        pair = (
            pltpu.make_async_copy(unit_hbm.at[rows], unit_ref.at[rows], sems.at[0, b]),
            pltpu.make_async_copy(match_hbm.at[rows], match_ref.at[rows], sems.at[1, b]),
        )
        for copy in pair:
            copy.start()
        copies.append(pair)
    ones = jnp.ones((total_ref.shape[0], sim_ref.shape[1]), bf16)
    scale = math.log2(math.e) / entropic_smoothing
    for b, pair in enumerate(copies):
        rows = pl.ds(b * TILE, TILE)
        for copy in pair:
            copy.wait()
        dots = lax.dot_general(
            unit_ref[rows, :], cent_ref[...], (((1,), (1,)), ((), ())), preferred_element_type=f32
        )
        sim = (jnp.exp2(dots * scale) * match_ref[rows, :].astype(f32)).astype(bf16)
        sim_ref[rows, :] = sim
        totals = lax.dot_general(ones, sim, (((1,), (1,)), ((), ())), preferred_element_type=f32)
        for q in range(TILE // LANES):
            total_ref[:, b * (TILE // LANES) + q, :] = totals[:, q * LANES : (q + 1) * LANES]


def column_kernel(parts_ref, sim_ref, out_ref):
    factor = 1.0 / jnp.sum(parts_ref[...], axis=0)
    lhs = two_terms(as_row(factor))
    sums = jnp.dot(lhs, sim_ref[...], preferred_element_type=f32)
    out_ref[...] = jnp.broadcast_to(as_tiles(jnp.sum(sums, axis=0, keepdims=True))[None], out_ref.shape)


def row_kernel(desired_load, parts_ref, sim_ref, out_ref):
    factor = desired_load / jnp.sum(parts_ref[...], axis=0)
    lhs = two_terms(as_row(factor))
    sums = lax.dot_general(lhs, sim_ref[...], (((1,), (1,)), ((), ())), preferred_element_type=f32)
    out_ref[...] = jnp.broadcast_to(as_tiles(jnp.sum(sums, axis=0, keepdims=True))[None], out_ref.shape)


def down(row):
    return jnp.transpose(jnp.broadcast_to(row, (LANES, LANES)))


def numerator_kernel(count, parts_ref, sim_ref, x_ref, out_ref, weight_ref):
    factor = 1.0 / jnp.sum(parts_ref[...], axis=0)
    lhs = two_terms(as_row(factor))
    mass = jnp.sum(jnp.dot(lhs, sim_ref[...], preferred_element_type=f32), axis=0, keepdims=True)
    columns = sim_ref.shape[1]
    for q in range(sim_ref.shape[0] // LANES):
        rows = pl.ds(q * LANES, LANES)
        scale = jnp.concatenate([down(factor[q : q + 1])] * (columns // LANES), axis=1)
        weight_ref[rows, :] = (sim_ref[rows, :].astype(f32) * scale).astype(bf16)
    chunks = x_ref.shape[1] // LANES
    held = columns // out_ref.shape[0]
    base = held * chunks
    for t in range(columns // TILE):
        sums = lax.dot_general(
            weight_ref[:, pl.ds(t * TILE, TILE)],
            x_ref[...],
            (((0,), (0,)), ((), ())),
            preferred_element_type=f32,
        ).astype(bf16)
        for z in range(TILE // count):
            slot, place = divmod(t * TILE + z * count, held)
            for c in range(chunks):
                out_ref[slot, pl.ds(place * chunks + c * count, count), :] = sums[
                    z * count : (z + 1) * count, c * LANES : (c + 1) * LANES
                ]
    for i in range(out_ref.shape[0]):
        own = as_tiles(mass[:, i * held : (i + 1) * held])
        rest = jnp.zeros((out_ref.shape[1] - base - own.shape[0], LANES), f32)
        out_ref[i, pl.ds(base, out_ref.shape[1] - base), :] = jnp.concatenate([own, rest], axis=0).astype(bf16)


def hand_on_kernel(count, parts_ref, out_ref):
    total = jnp.sum(parts_ref[...].astype(f32), axis=0)
    chunk_rows = out_ref.shape[1] - 16
    base = chunk_rows * out_ref.shape[0]
    for z in range(out_ref.shape[0]):
        out_ref[z, pl.ds(0, chunk_rows), :] = total[z * chunk_rows : (z + 1) * chunk_rows].astype(bf16)
        at = z * count % LANES
        row = total[base + z * count // LANES : base + z * count // LANES + 1]
        row = jnp.concatenate([row[:, at:], row[:, :at]], axis=1) if at else row
        out_ref[z, pl.ds(chunk_rows, 16), :] = jnp.broadcast_to(row, (16, LANES)).astype(bf16)


def update_kernel(parts_ref, cent_ref, out_ref):
    total = jnp.sum(parts_ref[...].astype(f32), axis=0)
    count, width = out_ref.shape
    chunk_rows = width // LANES * count
    scale = 1.0 / (down(total[chunk_rows : chunk_rows + 1])[:count] + 1.0)
    for c in range(width // LANES):
        lanes = pl.ds(c * LANES, LANES)
        out_ref[:, lanes] = (total[c * count : (c + 1) * count] + cent_ref[:, lanes]) * scale


def call(kernel, name, operands, outs, mib, flops, scratch=(), hbm_in=(), hbm_out=False):
    moved = sum(math.prod(o.shape) * o.dtype.itemsize for o in (*operands, *outs))
    vmem, hbm = pl.BlockSpec(memory_space=pltpu.VMEM), pl.BlockSpec(memory_space=pltpu.HBM)
    out = hbm if hbm_out else vmem
    single = len(outs) == 1
    if hbm_out:
        outs = [pltpu.HBM(o.shape, o.dtype) for o in outs]
    operands = [
        pltpu.with_memory_space_constraint(o, pltpu.HBM) if i in hbm_in else o
        for i, o in enumerate(operands)
    ]
    return pl.pallas_call(
        kernel,
        name=name,
        out_shape=outs[0] if single else outs,
        in_specs=[hbm if i in hbm_in else vmem for i in range(len(operands))],
        out_specs=out if single else [out] * len(outs),
        scratch_shapes=scratch,
        compiler_params=pltpu.CompilerParams(vmem_limit_bytes=mib * MIB),
        cost_estimate=pl.CostEstimate(flops=flops, bytes_accessed=moved, transcendentals=0),
    )(*operands)


def per_device(embeddings, coarse_ids, centroids, coarse_of):
    row_count, width = embeddings.shape
    local_count = centroids.shape[0]
    near, far, along_z = ("x", "zl"), "zh", ("zh", "zl")
    x_size, near_size, far_size = (lax.axis_size(axes) for axes in ("x", near, far))
    z_size = lax.axis_size(along_z)
    cent_size = lax.axis_size(("y", "core"))
    columns = x_size * z_size * local_count
    desired_load = row_count / (local_count * cent_size)
    layout_table = coarse_of.reshape(x_size, far_size, z_size // far_size, cent_size, local_count)
    group_ids = lax.dynamic_index_in_dim(
        layout_table, lax.axis_index(("y", "core")), 3, keepdims=False
    )
    group_ids = jnp.swapaxes(group_ids, 1, 2).reshape(1, columns)

    array = jax.ShapeDtypeStruct
    unit_like, match_like = array((row_count, width), bf16), array((row_count, columns), bf16)
    blocks = row_count // TILE
    unit_x, matched = call(
        prepare_kernel,
        "prepare",
        (embeddings, coarse_ids, group_ids),
        (unit_like, match_like),
        24,
        8 * row_count * CLUSTERS * columns,
        scratch=[
            pltpu.VMEM(unit_like.shape, bf16),
            pltpu.VMEM(match_like.shape, bf16),
            pltpu.VMEM((CLUSTERS, columns), bf16),
            pltpu.SemaphoreType.DMA((2, blocks)),
        ],
        hbm_out=True,
    )
    copies = call(
        unit_copies_kernel, "units", (centroids,), (array((far_size, local_count, width), bf16),), 4, 0
    )
    part = exchange(copies, far)
    copies = call(copies_kernel, "copies", (part,), (array((near_size,) + part.shape, bf16),), 4, 0)
    group_centroids = exchange(copies, near).reshape(columns, width)

    product = 2 * row_count * columns
    row_parts = array((cent_size, row_count // LANES, LANES), f32)
    column_parts = array((x_size, columns // LANES, LANES), f32)
    column_sums = array((z_size, columns // LANES, LANES), f32)
    similarity, parts = call(
        similarity_kernel,
        "similarity",
        (unit_x, group_centroids, matched),
        (match_like, row_parts),
        20,
        product * width,
        scratch=[
            pltpu.VMEM(unit_like.shape, bf16),
            pltpu.VMEM(match_like.shape, bf16),
            pltpu.SemaphoreType.DMA((2, blocks)),
        ],
        hbm_in=(0, 2),
    )
    parts = exchange(parts, ("y", "core"))
    for sweep in range(SWEEPS):
        parts = call(column_kernel, "columns", (parts, similarity), (column_parts,), 8, product * 16)
        parts = call(sum_copies_kernel, "across", (exchange(parts, "x"),), (column_sums,), 2, 0)
        parts = call(
            functools.partial(row_kernel, desired_load),
            "rows",
            (exchange(parts, along_z), similarity),
            (row_parts,),
            8,
            product * 16,
        )
        parts = exchange(parts, ("y", "core"))
    chunk_rows = width // LANES * local_count
    sums = call(
        functools.partial(numerator_kernel, local_count),
        "numerator",
        (parts, similarity, embeddings),
        (array((near_size, far_size * chunk_rows + 16, LANES), bf16),),
        16,
        product * width,
        scratch=[pltpu.VMEM((row_count, columns), bf16)],
    )
    sums = call(
        functools.partial(hand_on_kernel, local_count),
        "hand_on",
        (exchange(sums, near),),
        (array((far_size, chunk_rows + 16, LANES), bf16),),
        8,
        0,
    )
    return call(
        update_kernel,
        "update",
        (exchange(sums, far), centroids),
        (array(centroids.shape, f32),),
        4,
        0,
    )


def solution(mesh):
    fine = Mesh(mesh.devices.reshape(4, 8, 2, 4, 2), ("x", "zh", "zl", "y", "core"))
    rows, held = P(("x", "zh", "zl"), None), P(("x", "zh", "zl", "y", "core"), None)
    return jax.shard_map(
        per_device,
        mesh=fine,
        in_specs=(rows, rows, held, P()),
        out_specs=held,
        check_vma=False,
    )
```

```python
import functools
import math

import jax
import jax.numpy as jnp
from jax import lax
from jax.experimental import pallas as pl
from jax.experimental.pallas import tpu as pltpu
from jax.sharding import Mesh
from jax.sharding import PartitionSpec as P

SWEEPS = 3
CLUSTERS = 512
LANES = 128
TILE = 256


entropic_smoothing = 0.03
MIB = 1 << 20
f32, bf16 = jnp.float32, jnp.bfloat16


def unit_rows(values):
    values = values.astype(f32)
    return values * lax.rsqrt(jnp.sum(values * values, axis=-1, keepdims=True) + 1e-06)


def exchange(blocks, axes):
    return lax.all_to_all(blocks, axes, 0, 0)


def as_row(tiles):
    return jnp.concatenate([tiles[q : q + 1] for q in range(tiles.shape[0])], axis=1)


def as_tiles(row):
    count = row.shape[1] // LANES
    return jnp.concatenate([row[:, q * LANES : (q + 1) * LANES] for q in range(count)], axis=0)


def two_terms(row):
    wide = jnp.broadcast_to(row, (16, row.shape[1]))
    high = wide.astype(bf16).astype(f32)
    which = lax.broadcasted_iota(jnp.int32, wide.shape, 0)
    rest = jnp.where(which == 1, wide - high, 0.0)
    return jnp.where(which == 0, high, rest).astype(bf16)


def in_turn(blocks, copies, work, ahead=2):
    for b in range(min(ahead, blocks)):
        for copy in copies(b):
            copy.start()
    for b in range(blocks):
        if b + ahead < blocks:
            for copy in copies(b + ahead):
                copy.start()
        for copy in copies(b):
            copy.wait()
        work(b)


def prepare_kernel(x_hbm, ids_ref, group_ref, unit_hbm, match_hbm, x_ref, unit_ref, match_ref, hot_ref, sems):
    blocks = x_ref.shape[0] // TILE
    half = CLUSTERS // 2
    cluster = lax.broadcasted_iota(jnp.int32, hot_ref.shape, 0)
    hot_ref[...] = jnp.where(cluster == group_ref[...], 1.0, 0.0).astype(bf16)
    lane = lax.broadcasted_iota(jnp.int32, (TILE, half), 1).astype(f32).astype(bf16)

    def into(b):
        rows = pl.ds(b * TILE, TILE)
        return (pltpu.make_async_copy(x_hbm.at[rows], x_ref.at[rows], sems.at[0, b]),)

    def out_of(b):
        rows = pl.ds(b * TILE, TILE)
        return (
            pltpu.make_async_copy(unit_ref.at[rows], unit_hbm.at[rows], sems.at[1, b]),
            pltpu.make_async_copy(match_ref.at[rows], match_hbm.at[rows], sems.at[2, b]),
        )

    def work(b):
        rows = pl.ds(b * TILE, TILE)
        unit_ref[rows, :] = unit_rows(x_ref[rows, :]).astype(bf16)
        ids = ids_ref[rows, :]
        matched = jnp.zeros((TILE, match_ref.shape[1]), f32)
        for first in (0, half):
            near = (ids - first).astype(f32).astype(bf16)
            picked = jnp.zeros(lane.shape, bf16)
            for p in range(ids.shape[1]):
                picked = jnp.where(near[:, p : p + 1] == lane, jnp.ones_like(picked), picked)
            matched += jnp.dot(picked, hot_ref[first : first + half, :], preferred_element_type=f32)
        match_ref[rows, :] = matched.astype(bf16)
        for copy in out_of(b):
            copy.start()

    in_turn(blocks, into, work)
    for b in range(blocks):
        for copy in out_of(b):
            copy.wait()


def unit_copies_kernel(cent_ref, out_ref):
    out_ref[...] = jnp.broadcast_to(unit_rows(cent_ref[...]).astype(bf16)[None], out_ref.shape)


def copies_kernel(block_ref, out_ref):
    for i in range(out_ref.shape[0]):
        out_ref[i] = block_ref[...]


def sum_copies_kernel(parts_ref, out_ref):
    out_ref[...] = jnp.broadcast_to(jnp.sum(parts_ref[...], axis=0)[None], out_ref.shape)


def similarity_kernel(unit_hbm, cent_ref, match_hbm, sim_ref, total_ref, unit_ref, match_ref, sems):
    ones = jnp.ones((total_ref.shape[0], sim_ref.shape[1]), bf16)
    scale = math.log2(math.e) / entropic_smoothing

    def into(b):
        rows = pl.ds(b * TILE, TILE)
        return (
            pltpu.make_async_copy(unit_hbm.at[rows], unit_ref.at[rows], sems.at[0, b]),
            pltpu.make_async_copy(match_hbm.at[rows], match_ref.at[rows], sems.at[1, b]),
        )

    def work(b):
        rows = pl.ds(b * TILE, TILE)
        dots = lax.dot_general(
            unit_ref[rows, :], cent_ref[...], (((1,), (1,)), ((), ())), preferred_element_type=f32
        )
        sim = (jnp.exp2(dots * scale) * match_ref[rows, :].astype(f32)).astype(bf16)
        sim_ref[rows, :] = sim
        totals = lax.dot_general(ones, sim, (((1,), (1,)), ((), ())), preferred_element_type=f32)
        for q in range(TILE // LANES):
            total_ref[:, b * (TILE // LANES) + q, :] = totals[:, q * LANES : (q + 1) * LANES]

    in_turn(unit_ref.shape[0] // TILE, into, work)


def column_kernel(parts_ref, sim_ref, out_ref):
    factor = 1.0 / jnp.sum(parts_ref[...], axis=0)
    lhs = two_terms(as_row(factor))
    sums = jnp.dot(lhs, sim_ref[...], preferred_element_type=f32)
    out_ref[...] = jnp.broadcast_to(as_tiles(jnp.sum(sums, axis=0, keepdims=True))[None], out_ref.shape)


def row_kernel(desired_load, parts_ref, sim_ref, out_ref):
    factor = desired_load / jnp.sum(parts_ref[...], axis=0)
    lhs = two_terms(as_row(factor))
    sums = lax.dot_general(lhs, sim_ref[...], (((1,), (1,)), ((), ())), preferred_element_type=f32)
    out_ref[...] = jnp.broadcast_to(as_tiles(jnp.sum(sums, axis=0, keepdims=True))[None], out_ref.shape)


def down(row):
    return jnp.transpose(jnp.broadcast_to(row, (LANES, LANES)))


def numerator_kernel(count, parts_ref, sim_ref, x_ref, out_ref, weight_ref):
    factor = 1.0 / jnp.sum(parts_ref[...], axis=0)
    lhs = two_terms(as_row(factor))
    mass = jnp.sum(jnp.dot(lhs, sim_ref[...], preferred_element_type=f32), axis=0, keepdims=True)
    columns = sim_ref.shape[1]
    for q in range(sim_ref.shape[0] // LANES):
        rows = pl.ds(q * LANES, LANES)
        scale = jnp.concatenate([down(factor[q : q + 1])] * (columns // LANES), axis=1)
        weight_ref[rows, :] = (sim_ref[rows, :].astype(f32) * scale).astype(bf16)
    chunks = x_ref.shape[1] // LANES
    held = columns // out_ref.shape[0]
    base = held * chunks
    for t in range(columns // TILE):
        sums = lax.dot_general(
            weight_ref[:, pl.ds(t * TILE, TILE)],
            x_ref[...],
            (((0,), (0,)), ((), ())),
            preferred_element_type=f32,
        ).astype(bf16)
        for z in range(TILE // count):
            slot, place = divmod(t * TILE + z * count, held)
            for c in range(chunks):
                out_ref[slot, pl.ds(place * chunks + c * count, count), :] = sums[
                    z * count : (z + 1) * count, c * LANES : (c + 1) * LANES
                ]
    for i in range(out_ref.shape[0]):
        own = as_tiles(mass[:, i * held : (i + 1) * held])
        rest = jnp.zeros((out_ref.shape[1] - base - own.shape[0], LANES), f32)
        out_ref[i, pl.ds(base, out_ref.shape[1] - base), :] = jnp.concatenate([own, rest], axis=0).astype(bf16)


def hand_on_kernel(count, parts_ref, out_ref):
    total = jnp.sum(parts_ref[...].astype(f32), axis=0)
    chunk_rows = out_ref.shape[1] - 16
    base = chunk_rows * out_ref.shape[0]
    for z in range(out_ref.shape[0]):
        out_ref[z, pl.ds(0, chunk_rows), :] = total[z * chunk_rows : (z + 1) * chunk_rows].astype(bf16)
        at = z * count % LANES
        row = total[base + z * count // LANES : base + z * count // LANES + 1]
        row = jnp.concatenate([row[:, at:], row[:, :at]], axis=1) if at else row
        out_ref[z, pl.ds(chunk_rows, 16), :] = jnp.broadcast_to(row, (16, LANES)).astype(bf16)


def update_kernel(parts_ref, cent_ref, out_ref):
    total = jnp.sum(parts_ref[...].astype(f32), axis=0)
    count, width = out_ref.shape
    chunk_rows = width // LANES * count
    scale = 1.0 / (down(total[chunk_rows : chunk_rows + 1])[:count] + 1.0)
    for c in range(width // LANES):
        lanes = pl.ds(c * LANES, LANES)
        out_ref[:, lanes] = (total[c * count : (c + 1) * count] + cent_ref[:, lanes]) * scale


def call(kernel, name, operands, outs, mib, flops, scratch=(), hbm_in=(), hbm_out=False):
    moved = sum(math.prod(o.shape) * o.dtype.itemsize for o in (*operands, *outs))
    vmem, hbm = pl.BlockSpec(memory_space=pltpu.VMEM), pl.BlockSpec(memory_space=pltpu.HBM)
    out = hbm if hbm_out else vmem
    single = len(outs) == 1
    if hbm_out:
        outs = [pltpu.HBM(o.shape, o.dtype) for o in outs]
    operands = [
        pltpu.with_memory_space_constraint(o, pltpu.HBM) if i in hbm_in else o
        for i, o in enumerate(operands)
    ]
    return pl.pallas_call(
        kernel,
        name=name,
        out_shape=outs[0] if single else outs,
        in_specs=[hbm if i in hbm_in else vmem for i in range(len(operands))],
        out_specs=out if single else [out] * len(outs),
        scratch_shapes=scratch,
        compiler_params=pltpu.CompilerParams(vmem_limit_bytes=mib * MIB),
        cost_estimate=pl.CostEstimate(flops=flops, bytes_accessed=moved, transcendentals=0),
    )(*operands)


def per_device(embeddings, coarse_ids, centroids, coarse_of):
    row_count, width = embeddings.shape
    local_count = centroids.shape[0]
    near, far, along_z = ("x", "zl"), "zh", ("zh", "zl")
    x_size, near_size, far_size = (lax.axis_size(axes) for axes in ("x", near, far))
    z_size = lax.axis_size(along_z)
    cent_size = lax.axis_size(("y", "core"))
    columns = x_size * z_size * local_count
    desired_load = row_count / (local_count * cent_size)
    layout_table = coarse_of.reshape(x_size, far_size, z_size // far_size, cent_size, local_count)
    group_ids = lax.dynamic_index_in_dim(
        layout_table, lax.axis_index(("y", "core")), 3, keepdims=False
    )
    group_ids = jnp.swapaxes(group_ids, 1, 2).reshape(1, columns)

    array = jax.ShapeDtypeStruct
    unit_like, match_like = array((row_count, width), bf16), array((row_count, columns), bf16)
    blocks = row_count // TILE
    unit_x, matched = call(
        prepare_kernel,
        "prepare",
        (embeddings, coarse_ids, group_ids),
        (unit_like, match_like),
        24,
        8 * row_count * CLUSTERS * columns,
        scratch=[
            pltpu.VMEM(unit_like.shape, bf16),
            pltpu.VMEM(unit_like.shape, bf16),
            pltpu.VMEM(match_like.shape, bf16),
            pltpu.VMEM((CLUSTERS, columns), bf16),
            pltpu.SemaphoreType.DMA((3, blocks)),
        ],
        hbm_in=(0,),
        hbm_out=True,
    )
    copies = call(
        unit_copies_kernel, "units", (centroids,), (array((far_size, local_count, width), bf16),), 4, 0
    )
    part = exchange(copies, far)
    copies = call(copies_kernel, "copies", (part,), (array((near_size,) + part.shape, bf16),), 4, 0)
    group_centroids = exchange(copies, near).reshape(columns, width)

    product = 2 * row_count * columns
    row_parts = array((cent_size, row_count // LANES, LANES), f32)
    column_parts = array((x_size, columns // LANES, LANES), f32)
    column_sums = array((z_size, columns // LANES, LANES), f32)
    similarity, parts = call(
        similarity_kernel,
        "similarity",
        (unit_x, group_centroids, matched),
        (match_like, row_parts),
        20,
        product * width,
        scratch=[
            pltpu.VMEM(unit_like.shape, bf16),
            pltpu.VMEM(match_like.shape, bf16),
            pltpu.SemaphoreType.DMA((2, blocks)),
        ],
        hbm_in=(0, 2),
    )
    parts = exchange(parts, ("y", "core"))
    for sweep in range(SWEEPS):
        parts = call(column_kernel, "columns", (parts, similarity), (column_parts,), 8, product * 16)
        parts = call(sum_copies_kernel, "across", (exchange(parts, "x"),), (column_sums,), 2, 0)
        parts = call(
            functools.partial(row_kernel, desired_load),
            "rows",
            (exchange(parts, along_z), similarity),
            (row_parts,),
            8,
            product * 16,
        )
        parts = exchange(parts, ("y", "core"))
    chunk_rows = width // LANES * local_count
    sums = call(
        functools.partial(numerator_kernel, local_count),
        "numerator",
        (parts, similarity, embeddings),
        (array((near_size, far_size * chunk_rows + 16, LANES), bf16),),
        16,
        product * width,
        scratch=[pltpu.VMEM((row_count, columns), bf16)],
    )
    sums = call(
        functools.partial(hand_on_kernel, local_count),
        "hand_on",
        (exchange(sums, near),),
        (array((far_size, chunk_rows + 16, LANES), bf16),),
        8,
        0,
    )
    return call(
        update_kernel,
        "update",
        (exchange(sums, far), centroids),
        (array(centroids.shape, f32),),
        4,
        0,
    )


def solution(mesh):
    fine = Mesh(mesh.devices.reshape(4, 8, 2, 4, 2), ("x", "zh", "zl", "y", "core"))
    rows, held = P(("x", "zh", "zl"), None), P(("x", "zh", "zl", "y", "core"), None)
    return jax.shard_map(
        per_device,
        mesh=fine,
        in_specs=(rows, rows, held, P()),
        out_specs=held,
        check_vma=False,
    )
```

```python
import functools
import math

import jax
import jax.numpy as jnp
from jax import lax
from jax.experimental import pallas as pl
from jax.experimental.pallas import tpu as pltpu
from jax.sharding import Mesh
from jax.sharding import PartitionSpec as P

SWEEPS = 3
CLUSTERS = 512
LANES = 128
TILE = 256


entropic_smoothing = 0.03
MIB = 1 << 20
f32, bf16 = jnp.float32, jnp.bfloat16


def unit_rows(values):
    values = values.astype(f32)
    return values * lax.rsqrt(jnp.sum(values * values, axis=-1, keepdims=True) + 1e-06)


def exchange(blocks, axes):
    return lax.all_to_all(blocks, axes, 0, 0)


def as_row(tiles):
    return jnp.concatenate([tiles[q : q + 1] for q in range(tiles.shape[0])], axis=1)


def as_tiles(row):
    count = row.shape[1] // LANES
    return jnp.concatenate([row[:, q * LANES : (q + 1) * LANES] for q in range(count)], axis=0)


def two_terms(row):
    wide = jnp.broadcast_to(row, (16, row.shape[1]))
    high = wide.astype(bf16).astype(f32)
    which = lax.broadcasted_iota(jnp.int32, wide.shape, 0)
    rest = jnp.where(which == 1, wide - high, 0.0)
    return jnp.where(which == 0, high, rest).astype(bf16)


def in_turn(blocks, copies, work, ahead=2):
    for b in range(min(ahead, blocks)):
        for copy in copies(b):
            copy.start()
    for b in range(blocks):
        if b + ahead < blocks:
            for copy in copies(b + ahead):
                copy.start()
        for copy in copies(b):
            copy.wait()
        work(b)


def prepare_kernel(x_hbm, ids_ref, group_ref, unit_hbm, match_hbm, x_ref, unit_ref, match_ref, hot_ref, sems):
    blocks = x_ref.shape[0] // TILE
    half = CLUSTERS // 2
    cluster = lax.broadcasted_iota(jnp.int32, hot_ref.shape, 0)
    hot_ref[...] = jnp.where(cluster == group_ref[...], 1.0, 0.0).astype(bf16)
    lane = lax.broadcasted_iota(jnp.int32, (TILE, half), 1).astype(f32).astype(bf16)

    def into(b):
        rows = pl.ds(b * TILE, TILE)
        return (pltpu.make_async_copy(x_hbm.at[rows], x_ref.at[rows], sems.at[0, b]),)

    def out_of(b):
        rows = pl.ds(b * TILE, TILE)
        return (
            pltpu.make_async_copy(unit_ref.at[rows], unit_hbm.at[rows], sems.at[1, b]),
            pltpu.make_async_copy(match_ref.at[rows], match_hbm.at[rows], sems.at[2, b]),
        )

    def work(b):
        rows = pl.ds(b * TILE, TILE)
        unit_ref[rows, :] = unit_rows(x_ref[rows, :]).astype(bf16)
        ids = ids_ref[rows, :]
        matched = jnp.zeros((TILE, match_ref.shape[1]), f32)
        for first in (0, half):
            near = (ids - first).astype(f32).astype(bf16)
            picked = jnp.zeros(lane.shape, bf16)
            for p in range(ids.shape[1]):
                picked = jnp.where(near[:, p : p + 1] == lane, jnp.ones_like(picked), picked)
            matched += jnp.dot(picked, hot_ref[first : first + half, :], preferred_element_type=f32)
        match_ref[rows, :] = matched.astype(bf16)
        for copy in out_of(b):
            copy.start()

    in_turn(blocks, into, work)
    for b in range(blocks):
        for copy in out_of(b):
            copy.wait()


def unit_copies_kernel(cent_ref, out_ref):
    out_ref[...] = jnp.broadcast_to(unit_rows(cent_ref[...]).astype(bf16)[None], out_ref.shape)


def copies_kernel(block_ref, unused, out_ref):
    for i in range(out_ref.shape[0]):
        out_ref[i] = block_ref[...]


def sum_copies_kernel(parts_ref, out_ref):
    out_ref[...] = jnp.broadcast_to(jnp.sum(parts_ref[...], axis=0)[None], out_ref.shape)


def similarity_kernel(unit_ref, cent_ref, match_ref, sim_ref, total_ref):
    ones = jnp.ones((total_ref.shape[0], sim_ref.shape[1]), bf16)
    scale = math.log2(math.e) / entropic_smoothing
    for b in range(unit_ref.shape[0] // TILE):
        rows = pl.ds(b * TILE, TILE)
        dots = lax.dot_general(
            unit_ref[rows, :], cent_ref[...], (((1,), (1,)), ((), ())), preferred_element_type=f32
        )
        sim = (jnp.exp2(dots * scale) * match_ref[rows, :].astype(f32)).astype(bf16)
        sim_ref[rows, :] = sim
        totals = lax.dot_general(ones, sim, (((1,), (1,)), ((), ())), preferred_element_type=f32)
        for q in range(TILE // LANES):
            total_ref[:, b * (TILE // LANES) + q, :] = totals[:, q * LANES : (q + 1) * LANES]


def column_kernel(parts_ref, sim_ref, out_ref):
    factor = 1.0 / jnp.sum(parts_ref[...], axis=0)
    lhs = two_terms(as_row(factor))
    sums = jnp.dot(lhs, sim_ref[...], preferred_element_type=f32)
    out_ref[...] = jnp.broadcast_to(as_tiles(jnp.sum(sums, axis=0, keepdims=True))[None], out_ref.shape)


def row_kernel(desired_load, parts_ref, sim_ref, out_ref):
    factor = desired_load / jnp.sum(parts_ref[...], axis=0)
    lhs = two_terms(as_row(factor))
    sums = lax.dot_general(lhs, sim_ref[...], (((1,), (1,)), ((), ())), preferred_element_type=f32)
    out_ref[...] = jnp.broadcast_to(as_tiles(jnp.sum(sums, axis=0, keepdims=True))[None], out_ref.shape)


def down(row):
    return jnp.transpose(jnp.broadcast_to(row, (LANES, LANES)))


def numerator_kernel(count, parts_ref, sim_ref, x_ref, out_ref, weight_ref):
    factor = 1.0 / jnp.sum(parts_ref[...], axis=0)
    lhs = two_terms(as_row(factor))
    mass = jnp.sum(jnp.dot(lhs, sim_ref[...], preferred_element_type=f32), axis=0, keepdims=True)
    columns = sim_ref.shape[1]
    for q in range(sim_ref.shape[0] // LANES):
        rows = pl.ds(q * LANES, LANES)
        scale = jnp.concatenate([down(factor[q : q + 1])] * (columns // LANES), axis=1)
        weight_ref[rows, :] = (sim_ref[rows, :].astype(f32) * scale).astype(bf16)
    chunks = x_ref.shape[1] // LANES
    held = columns // out_ref.shape[0]
    base = held * chunks
    for t in range(columns // TILE):
        sums = lax.dot_general(
            weight_ref[:, pl.ds(t * TILE, TILE)],
            x_ref[...],
            (((0,), (0,)), ((), ())),
            preferred_element_type=f32,
        ).astype(bf16)
        for z in range(TILE // count):
            slot, place = divmod(t * TILE + z * count, held)
            for c in range(chunks):
                out_ref[slot, pl.ds(place * chunks + c * count, count), :] = sums[
                    z * count : (z + 1) * count, c * LANES : (c + 1) * LANES
                ]
    for i in range(out_ref.shape[0]):
        own = as_tiles(mass[:, i * held : (i + 1) * held])
        rest = jnp.zeros((out_ref.shape[1] - base - own.shape[0], LANES), f32)
        out_ref[i, pl.ds(base, out_ref.shape[1] - base), :] = jnp.concatenate([own, rest], axis=0).astype(bf16)


def hand_on_kernel(count, parts_ref, out_ref):
    total = jnp.sum(parts_ref[...].astype(f32), axis=0)
    chunk_rows = out_ref.shape[1] - 16
    base = chunk_rows * out_ref.shape[0]
    for z in range(out_ref.shape[0]):
        out_ref[z, pl.ds(0, chunk_rows), :] = total[z * chunk_rows : (z + 1) * chunk_rows].astype(bf16)
        at = z * count % LANES
        row = total[base + z * count // LANES : base + z * count // LANES + 1]
        row = jnp.concatenate([row[:, at:], row[:, :at]], axis=1) if at else row
        out_ref[z, pl.ds(chunk_rows, 16), :] = jnp.broadcast_to(row, (16, LANES)).astype(bf16)


def update_kernel(parts_ref, cent_ref, out_ref):
    total = jnp.sum(parts_ref[...].astype(f32), axis=0)
    count, width = out_ref.shape
    chunk_rows = width // LANES * count
    scale = 1.0 / (down(total[chunk_rows : chunk_rows + 1])[:count] + 1.0)
    for c in range(width // LANES):
        lanes = pl.ds(c * LANES, LANES)
        out_ref[:, lanes] = (total[c * count : (c + 1) * count] + cent_ref[:, lanes]) * scale


def call(kernel, name, operands, outs, mib, flops, scratch=(), hbm_in=(), hbm_out=False):
    moved = sum(math.prod(o.shape) * o.dtype.itemsize for o in (*operands, *outs))
    vmem, hbm = pl.BlockSpec(memory_space=pltpu.VMEM), pl.BlockSpec(memory_space=pltpu.HBM)
    out = hbm if hbm_out else vmem
    single = len(outs) == 1
    if hbm_out:
        outs = [pltpu.HBM(o.shape, o.dtype) for o in outs]
    operands = [
        pltpu.with_memory_space_constraint(o, pltpu.HBM) if i in hbm_in else o
        for i, o in enumerate(operands)
    ]
    return pl.pallas_call(
        kernel,
        name=name,
        out_shape=outs[0] if single else outs,
        in_specs=[hbm if i in hbm_in else vmem for i in range(len(operands))],
        out_specs=out if single else [out] * len(outs),
        scratch_shapes=scratch,
        compiler_params=pltpu.CompilerParams(vmem_limit_bytes=mib * MIB),
        cost_estimate=pl.CostEstimate(flops=flops, bytes_accessed=moved, transcendentals=0),
    )(*operands)


def per_device(embeddings, coarse_ids, centroids, coarse_of):
    row_count, width = embeddings.shape
    local_count = centroids.shape[0]
    near, far, along_z = ("x", "zl"), "zh", ("zh", "zl")
    x_size, near_size, far_size = (lax.axis_size(axes) for axes in ("x", near, far))
    z_size = lax.axis_size(along_z)
    cent_size = lax.axis_size(("y", "core"))
    columns = x_size * z_size * local_count
    desired_load = row_count / (local_count * cent_size)
    layout_table = coarse_of.reshape(x_size, far_size, z_size // far_size, cent_size, local_count)
    group_ids = lax.dynamic_index_in_dim(
        layout_table, lax.axis_index(("y", "core")), 3, keepdims=False
    )
    group_ids = jnp.swapaxes(group_ids, 1, 2).reshape(1, columns)

    array = jax.ShapeDtypeStruct
    unit_like, match_like = array((row_count, width), bf16), array((row_count, columns), bf16)
    blocks = row_count // TILE
    unit_x, matched = call(
        prepare_kernel,
        "prepare",
        (embeddings, coarse_ids, group_ids),
        (unit_like, match_like),
        24,
        8 * row_count * CLUSTERS * columns,
        scratch=[
            pltpu.VMEM(unit_like.shape, bf16),
            pltpu.VMEM(unit_like.shape, bf16),
            pltpu.VMEM(match_like.shape, bf16),
            pltpu.VMEM((CLUSTERS, columns), bf16),
            pltpu.SemaphoreType.DMA((3, blocks)),
        ],
        hbm_in=(0,),
        hbm_out=True,
    )
    copies = call(
        unit_copies_kernel, "units", (centroids,), (array((far_size, local_count, width), bf16),), 4, 0
    )
    part = exchange(copies, far)
    copies = call(
        copies_kernel,
        "copies",
        (part, matched),
        (array((near_size,) + part.shape, bf16),),
        4,
        0,
        hbm_in=(1,),
    )
    group_centroids = exchange(copies, near).reshape(columns, width)

    product = 2 * row_count * columns
    row_parts = array((cent_size, row_count // LANES, LANES), f32)
    column_parts = array((x_size, columns // LANES, LANES), f32)
    column_sums = array((z_size, columns // LANES, LANES), f32)
    similarity, parts = call(
        similarity_kernel,
        "similarity",
        (unit_x, group_centroids, matched),
        (match_like, row_parts),
        16,
        product * width,
    )
    parts = exchange(parts, ("y", "core"))
    for sweep in range(SWEEPS):
        parts = call(column_kernel, "columns", (parts, similarity), (column_parts,), 8, product * 16)
        parts = call(sum_copies_kernel, "across", (exchange(parts, "x"),), (column_sums,), 2, 0)
        parts = call(
            functools.partial(row_kernel, desired_load),
            "rows",
            (exchange(parts, along_z), similarity),
            (row_parts,),
            8,
            product * 16,
        )
        parts = exchange(parts, ("y", "core"))
    chunk_rows = width // LANES * local_count
    sums = call(
        functools.partial(numerator_kernel, local_count),
        "numerator",
        (parts, similarity, embeddings),
        (array((near_size, far_size * chunk_rows + 16, LANES), bf16),),
        16,
        product * width,
        scratch=[pltpu.VMEM((row_count, columns), bf16)],
    )
    sums = call(
        functools.partial(hand_on_kernel, local_count),
        "hand_on",
        (exchange(sums, near),),
        (array((far_size, chunk_rows + 16, LANES), bf16),),
        8,
        0,
    )
    return call(
        update_kernel,
        "update",
        (exchange(sums, far), centroids),
        (array(centroids.shape, f32),),
        4,
        0,
    )


def solution(mesh):
    fine = Mesh(mesh.devices.reshape(4, 8, 2, 4, 2), ("x", "zh", "zl", "y", "core"))
    rows, held = P(("x", "zh", "zl"), None), P(("x", "zh", "zl", "y", "core"), None)
    return jax.shard_map(
        per_device,
        mesh=fine,
        in_specs=(rows, rows, held, P()),
        out_specs=held,
        check_vma=False,
    )
```

```python
import functools
import math

import jax
import jax.numpy as jnp
from jax import lax
from jax.experimental import pallas as pl
from jax.experimental.pallas import tpu as pltpu
from jax.sharding import Mesh
from jax.sharding import PartitionSpec as P

SWEEPS = 3
CLUSTERS = 512
LANES = 128
TILE = 256


entropic_smoothing = 0.03
MIB = 1 << 20
f32, bf16 = jnp.float32, jnp.bfloat16


def unit_rows(values):
    values = values.astype(f32)
    return values * lax.rsqrt(jnp.sum(values * values, axis=-1, keepdims=True) + 1e-06)


def exchange(blocks, axes):
    return lax.all_to_all(blocks, axes, 0, 0)


def as_row(tiles):
    return jnp.concatenate([tiles[q : q + 1] for q in range(tiles.shape[0])], axis=1)


def as_tiles(row):
    count = row.shape[1] // LANES
    return jnp.concatenate([row[:, q * LANES : (q + 1) * LANES] for q in range(count)], axis=0)


def two_terms(row):
    wide = jnp.broadcast_to(row, (16, row.shape[1]))
    high = wide.astype(bf16).astype(f32)
    which = lax.broadcasted_iota(jnp.int32, wide.shape, 0)
    rest = jnp.where(which == 1, wide - high, 0.0)
    return jnp.where(which == 0, high, rest).astype(bf16)


def in_turn(blocks, copies, work, ahead=2):
    for b in range(min(ahead, blocks)):
        for copy in copies(b):
            copy.start()
    for b in range(blocks):
        if b + ahead < blocks:
            for copy in copies(b + ahead):
                copy.start()
        for copy in copies(b):
            copy.wait()
        work(b)


def prepare_kernel(x_hbm, ids_ref, group_ref, unit_hbm, match_hbm, x_ref, unit_ref, match_ref, hot_ref, sems):
    blocks = x_ref.shape[0] // TILE
    half = CLUSTERS // 2
    cluster = lax.broadcasted_iota(jnp.int32, hot_ref.shape, 0)
    hot_ref[...] = jnp.where(cluster == group_ref[...], 1.0, 0.0).astype(bf16)
    lane = lax.broadcasted_iota(jnp.int32, (TILE, half), 1).astype(f32).astype(bf16)

    def into(b):
        rows = pl.ds(b * TILE, TILE)
        return (pltpu.make_async_copy(x_hbm.at[rows], x_ref.at[rows], sems.at[0, b]),)

    def out_of(b):
        rows = pl.ds(b * TILE, TILE)
        return (
            pltpu.make_async_copy(unit_ref.at[rows], unit_hbm.at[rows], sems.at[1, b]),
            pltpu.make_async_copy(match_ref.at[rows], match_hbm.at[rows], sems.at[2, b]),
        )

    def work(b):
        rows = pl.ds(b * TILE, TILE)
        unit_ref[rows, :] = unit_rows(x_ref[rows, :]).astype(bf16)
        ids = ids_ref[rows, :]
        matched = jnp.zeros((TILE, match_ref.shape[1]), f32)
        for first in (0, half):
            near = (ids - first).astype(f32).astype(bf16)
            picked = jnp.zeros(lane.shape, bf16)
            for p in range(ids.shape[1]):
                picked = jnp.where(near[:, p : p + 1] == lane, jnp.ones_like(picked), picked)
            matched += jnp.dot(picked, hot_ref[first : first + half, :], preferred_element_type=f32)
        match_ref[rows, :] = matched.astype(bf16)
        for copy in out_of(b):
            copy.start()

    in_turn(blocks, into, work)
    for b in range(blocks):
        for copy in out_of(b):
            copy.wait()


def unit_copies_kernel(cent_ref, out_ref):
    out_ref[...] = jnp.broadcast_to(unit_rows(cent_ref[...]).astype(bf16)[None], out_ref.shape)


def copies_kernel(block_ref, unused, out_ref):
    for i in range(out_ref.shape[0]):
        out_ref[i] = block_ref[...]


def sum_copies_kernel(parts_ref, out_ref):
    out_ref[...] = jnp.broadcast_to(jnp.sum(parts_ref[...], axis=0)[None], out_ref.shape)


def similarity_kernel(unit_hbm, cent_ref, match_hbm, sim_ref, total_ref, unit_ref, match_ref, sems):
    ones = jnp.ones((total_ref.shape[0], sim_ref.shape[1]), bf16)
    scale = math.log2(math.e) / entropic_smoothing
    total_rows = unit_ref.shape[0]
    starts = [0, TILE] + list(range(2 * TILE, total_rows, 2 * TILE))
    spans = [pl.ds(i, j - i) for i, j in zip(starts, starts[1:] + [total_rows])]

    def into(b):
        rows = spans[b]
        return (
            pltpu.make_async_copy(unit_hbm.at[rows], unit_ref.at[rows], sems.at[0, b]),
            pltpu.make_async_copy(match_hbm.at[rows], match_ref.at[rows], sems.at[1, b]),
        )

    def work(b):
        for first in range(starts[b], starts[b] + spans[b].size, TILE):
            rows = pl.ds(first, TILE)
            dots = lax.dot_general(
                unit_ref[rows, :], cent_ref[...], (((1,), (1,)), ((), ())), preferred_element_type=f32
            )
            sim = (jnp.exp2(dots * scale) * match_ref[rows, :].astype(f32)).astype(bf16)
            sim_ref[rows, :] = sim
            totals = lax.dot_general(ones, sim, (((1,), (1,)), ((), ())), preferred_element_type=f32)
            for q in range(TILE // LANES):
                total_ref[:, first // LANES + q, :] = totals[:, q * LANES : (q + 1) * LANES]

    in_turn(len(spans), into, work, ahead=3)


def column_kernel(parts_ref, sim_ref, out_ref):
    factor = 1.0 / jnp.sum(parts_ref[...], axis=0)
    lhs = two_terms(as_row(factor))
    sums = jnp.dot(lhs, sim_ref[...], preferred_element_type=f32)
    out_ref[...] = jnp.broadcast_to(as_tiles(jnp.sum(sums, axis=0, keepdims=True))[None], out_ref.shape)


def row_kernel(desired_load, parts_ref, sim_ref, out_ref):
    factor = desired_load / jnp.sum(parts_ref[...], axis=0)
    lhs = two_terms(as_row(factor))
    sums = lax.dot_general(lhs, sim_ref[...], (((1,), (1,)), ((), ())), preferred_element_type=f32)
    out_ref[...] = jnp.broadcast_to(as_tiles(jnp.sum(sums, axis=0, keepdims=True))[None], out_ref.shape)


def down(row):
    return jnp.transpose(jnp.broadcast_to(row, (LANES, LANES)))


def numerator_kernel(count, parts_ref, sim_ref, x_ref, out_ref, weight_ref):
    factor = 1.0 / jnp.sum(parts_ref[...], axis=0)
    lhs = two_terms(as_row(factor))
    mass = jnp.sum(jnp.dot(lhs, sim_ref[...], preferred_element_type=f32), axis=0, keepdims=True)
    columns = sim_ref.shape[1]
    for q in range(sim_ref.shape[0] // LANES):
        rows = pl.ds(q * LANES, LANES)
        scale = jnp.concatenate([down(factor[q : q + 1])] * (columns // LANES), axis=1)
        weight_ref[rows, :] = (sim_ref[rows, :].astype(f32) * scale).astype(bf16)
    chunks = x_ref.shape[1] // LANES
    held = columns // out_ref.shape[0]
    base = held * chunks
    for t in range(columns // TILE):
        sums = lax.dot_general(
            weight_ref[:, pl.ds(t * TILE, TILE)],
            x_ref[...],
            (((0,), (0,)), ((), ())),
            preferred_element_type=f32,
        ).astype(bf16)
        for z in range(TILE // count):
            slot, place = divmod(t * TILE + z * count, held)
            for c in range(chunks):
                out_ref[slot, pl.ds(place * chunks + c * count, count), :] = sums[
                    z * count : (z + 1) * count, c * LANES : (c + 1) * LANES
                ]
    for i in range(out_ref.shape[0]):
        own = as_tiles(mass[:, i * held : (i + 1) * held])
        rest = jnp.zeros((out_ref.shape[1] - base - own.shape[0], LANES), f32)
        out_ref[i, pl.ds(base, out_ref.shape[1] - base), :] = jnp.concatenate([own, rest], axis=0).astype(bf16)


def hand_on_kernel(count, parts_ref, out_ref):
    total = jnp.sum(parts_ref[...].astype(f32), axis=0)
    chunk_rows = out_ref.shape[1] - 16
    base = chunk_rows * out_ref.shape[0]
    for z in range(out_ref.shape[0]):
        out_ref[z, pl.ds(0, chunk_rows), :] = total[z * chunk_rows : (z + 1) * chunk_rows].astype(bf16)
        at = z * count % LANES
        row = total[base + z * count // LANES : base + z * count // LANES + 1]
        row = jnp.concatenate([row[:, at:], row[:, :at]], axis=1) if at else row
        out_ref[z, pl.ds(chunk_rows, 16), :] = jnp.broadcast_to(row, (16, LANES)).astype(bf16)


def update_kernel(parts_ref, cent_ref, out_ref):
    total = jnp.sum(parts_ref[...].astype(f32), axis=0)
    count, width = out_ref.shape
    chunk_rows = width // LANES * count
    scale = 1.0 / (down(total[chunk_rows : chunk_rows + 1])[:count] + 1.0)
    for c in range(width // LANES):
        lanes = pl.ds(c * LANES, LANES)
        out_ref[:, lanes] = (total[c * count : (c + 1) * count] + cent_ref[:, lanes]) * scale


def call(kernel, name, operands, outs, mib, flops, scratch=(), hbm_in=(), hbm_out=False):
    moved = sum(math.prod(o.shape) * o.dtype.itemsize for o in (*operands, *outs))
    vmem, hbm = pl.BlockSpec(memory_space=pltpu.VMEM), pl.BlockSpec(memory_space=pltpu.HBM)
    out = hbm if hbm_out else vmem
    single = len(outs) == 1
    if hbm_out:
        outs = [pltpu.HBM(o.shape, o.dtype) for o in outs]
    operands = [
        pltpu.with_memory_space_constraint(o, pltpu.HBM) if i in hbm_in else o
        for i, o in enumerate(operands)
    ]
    return pl.pallas_call(
        kernel,
        name=name,
        out_shape=outs[0] if single else outs,
        in_specs=[hbm if i in hbm_in else vmem for i in range(len(operands))],
        out_specs=out if single else [out] * len(outs),
        scratch_shapes=scratch,
        compiler_params=pltpu.CompilerParams(vmem_limit_bytes=mib * MIB),
        cost_estimate=pl.CostEstimate(flops=flops, bytes_accessed=moved, transcendentals=0),
    )(*operands)


def per_device(embeddings, coarse_ids, centroids, coarse_of):
    row_count, width = embeddings.shape
    local_count = centroids.shape[0]
    near, far, along_z = ("x", "zl"), "zh", ("zh", "zl")
    x_size, near_size, far_size = (lax.axis_size(axes) for axes in ("x", near, far))
    z_size = lax.axis_size(along_z)
    cent_size = lax.axis_size(("y", "core"))
    columns = x_size * z_size * local_count
    desired_load = row_count / (local_count * cent_size)
    layout_table = coarse_of.reshape(x_size, far_size, z_size // far_size, cent_size, local_count)
    group_ids = lax.dynamic_index_in_dim(
        layout_table, lax.axis_index(("y", "core")), 3, keepdims=False
    )
    group_ids = jnp.swapaxes(group_ids, 1, 2).reshape(1, columns)

    array = jax.ShapeDtypeStruct
    unit_like, match_like = array((row_count, width), bf16), array((row_count, columns), bf16)
    blocks = row_count // TILE
    unit_x, matched = call(
        prepare_kernel,
        "prepare",
        (embeddings, coarse_ids, group_ids),
        (unit_like, match_like),
        24,
        8 * row_count * CLUSTERS * columns,
        scratch=[
            pltpu.VMEM(unit_like.shape, bf16),
            pltpu.VMEM(unit_like.shape, bf16),
            pltpu.VMEM(match_like.shape, bf16),
            pltpu.VMEM((CLUSTERS, columns), bf16),
            pltpu.SemaphoreType.DMA((3, blocks)),
        ],
        hbm_in=(0,),
        hbm_out=True,
    )
    copies = call(
        unit_copies_kernel, "units", (centroids,), (array((far_size, local_count, width), bf16),), 4, 0
    )
    part = exchange(copies, far)
    copies = call(
        copies_kernel,
        "copies",
        (part, matched),
        (array((near_size,) + part.shape, bf16),),
        4,
        0,
        hbm_in=(1,),
    )
    group_centroids = exchange(copies, near).reshape(columns, width)

    product = 2 * row_count * columns
    row_parts = array((cent_size, row_count // LANES, LANES), f32)
    column_parts = array((x_size, columns // LANES, LANES), f32)
    column_sums = array((z_size, columns // LANES, LANES), f32)
    similarity, parts = call(
        similarity_kernel,
        "similarity",
        (unit_x, group_centroids, matched),
        (match_like, row_parts),
        20,
        product * width,
        scratch=[
            pltpu.VMEM(unit_like.shape, bf16),
            pltpu.VMEM(match_like.shape, bf16),
            pltpu.SemaphoreType.DMA((2, blocks)),
        ],
        hbm_in=(0, 2),
    )
    parts = exchange(parts, ("y", "core"))
    for sweep in range(SWEEPS):
        parts = call(column_kernel, "columns", (parts, similarity), (column_parts,), 8, product * 16)
        parts = call(sum_copies_kernel, "across", (exchange(parts, "x"),), (column_sums,), 2, 0)
        parts = call(
            functools.partial(row_kernel, desired_load),
            "rows",
            (exchange(parts, along_z), similarity),
            (row_parts,),
            8,
            product * 16,
        )
        parts = exchange(parts, ("y", "core"))
    chunk_rows = width // LANES * local_count
    sums = call(
        functools.partial(numerator_kernel, local_count),
        "numerator",
        (parts, similarity, embeddings),
        (array((near_size, far_size * chunk_rows + 16, LANES), bf16),),
        16,
        product * width,
        scratch=[pltpu.VMEM((row_count, columns), bf16)],
    )
    sums = call(
        functools.partial(hand_on_kernel, local_count),
        "hand_on",
        (exchange(sums, near),),
        (array((far_size, chunk_rows + 16, LANES), bf16),),
        8,
        0,
    )
    return call(
        update_kernel,
        "update",
        (exchange(sums, far), centroids),
        (array(centroids.shape, f32),),
        4,
        0,
    )


def solution(mesh):
    fine = Mesh(mesh.devices.reshape(4, 8, 2, 4, 2), ("x", "zh", "zl", "y", "core"))
    rows, held = P(("x", "zh", "zl"), None), P(("x", "zh", "zl", "y", "core"), None)
    return jax.shard_map(
        per_device,
        mesh=fine,
        in_specs=(rows, rows, held, P()),
        out_specs=held,
        check_vma=False,
    )
```

```python
import functools
import math

import jax
import jax.numpy as jnp
from jax import lax
from jax.experimental import pallas as pl
from jax.experimental.pallas import tpu as pltpu
from jax.sharding import Mesh
from jax.sharding import PartitionSpec as P

SWEEPS = 3
CLUSTERS = 512
LANES = 128
TILE = 256


entropic_smoothing = 0.03
MIB = 1 << 20
f32, bf16 = jnp.float32, jnp.bfloat16


def unit_rows(values):
    values = values.astype(f32)
    return values * lax.rsqrt(jnp.sum(values * values, axis=-1, keepdims=True) + 1e-06)


def exchange(blocks, axes):
    return lax.all_to_all(blocks, axes, 0, 0)


def as_row(tiles):
    return jnp.concatenate([tiles[q : q + 1] for q in range(tiles.shape[0])], axis=1)


def as_tiles(row):
    count = row.shape[1] // LANES
    return jnp.concatenate([row[:, q * LANES : (q + 1) * LANES] for q in range(count)], axis=0)


def two_terms(row):
    wide = jnp.broadcast_to(row, (16, row.shape[1]))
    high = wide.astype(bf16).astype(f32)
    which = lax.broadcasted_iota(jnp.int32, wide.shape, 0)
    rest = jnp.where(which == 1, wide - high, 0.0)
    return jnp.where(which == 0, high, rest).astype(bf16)


def in_turn(blocks, copies, work, ahead=2):
    for b in range(min(ahead, blocks)):
        for copy in copies(b):
            copy.start()
    for b in range(blocks):
        if b + ahead < blocks:
            for copy in copies(b + ahead):
                copy.start()
        for copy in copies(b):
            copy.wait()
        work(b)


def prepare_kernel(x_hbm, ids_ref, group_ref, unit_hbm, match_hbm, x_ref, unit_ref, match_ref, hot_ref, sems):
    blocks = x_ref.shape[0] // TILE
    half = CLUSTERS // 2
    cluster = lax.broadcasted_iota(jnp.int32, hot_ref.shape, 0)
    hot_ref[...] = jnp.where(cluster == group_ref[...], 1.0, 0.0).astype(bf16)
    lane = lax.broadcasted_iota(jnp.int32, (TILE, half), 1).astype(f32).astype(bf16)

    def into(b):
        rows = pl.ds(b * TILE, TILE)
        return (pltpu.make_async_copy(x_hbm.at[rows], x_ref.at[rows], sems.at[0, b]),)

    def out_of(b):
        rows = pl.ds(b * TILE, TILE)
        return (
            pltpu.make_async_copy(unit_ref.at[rows], unit_hbm.at[rows], sems.at[1, b]),
            pltpu.make_async_copy(match_ref.at[rows], match_hbm.at[rows], sems.at[2, b]),
        )

    def work(b):
        rows = pl.ds(b * TILE, TILE)
        unit_ref[rows, :] = unit_rows(x_ref[rows, :]).astype(bf16)
        ids = ids_ref[rows, :]
        matched = jnp.zeros((TILE, match_ref.shape[1]), f32)
        for first in (0, half):
            near = (ids - first).astype(f32).astype(bf16)
            picked = jnp.zeros(lane.shape, bf16)
            for p in range(ids.shape[1]):
                picked = jnp.where(near[:, p : p + 1] == lane, jnp.ones_like(picked), picked)
            matched += jnp.dot(picked, hot_ref[first : first + half, :], preferred_element_type=f32)
        match_ref[rows, :] = matched.astype(bf16)
        for copy in out_of(b):
            copy.start()

    in_turn(blocks, into, work)
    for b in range(blocks):
        for copy in out_of(b):
            copy.wait()


def unit_copies_kernel(cent_ref, out_ref):
    out_ref[...] = jnp.broadcast_to(unit_rows(cent_ref[...]).astype(bf16)[None], out_ref.shape)


def copies_kernel(block_ref, out_ref):
    for i in range(out_ref.shape[0]):
        out_ref[i] = block_ref[...]


def sum_copies_kernel(parts_ref, out_ref):
    out_ref[...] = jnp.broadcast_to(jnp.sum(parts_ref[...], axis=0)[None], out_ref.shape)


def similarity_kernel(unit_hbm, cent_ref, match_hbm, sim_ref, total_ref, unit_ref, match_ref, sems):
    ones = jnp.ones((total_ref.shape[0], sim_ref.shape[1]), bf16)
    scale = math.log2(math.e) / entropic_smoothing
    total_rows = unit_ref.shape[0]
    starts = [0, TILE] + list(range(2 * TILE, total_rows, 2 * TILE))
    spans = [pl.ds(i, j - i) for i, j in zip(starts, starts[1:] + [total_rows])]

    def into(b):
        rows = spans[b]
        return (
            pltpu.make_async_copy(unit_hbm.at[rows], unit_ref.at[rows], sems.at[0, b]),
            pltpu.make_async_copy(match_hbm.at[rows], match_ref.at[rows], sems.at[1, b]),
        )

    def work(b):
        for first in range(starts[b], starts[b] + spans[b].size, TILE):
            rows = pl.ds(first, TILE)
            dots = lax.dot_general(
                unit_ref[rows, :], cent_ref[...], (((1,), (1,)), ((), ())), preferred_element_type=f32
            )
            sim = (jnp.exp2(dots * scale) * match_ref[rows, :].astype(f32)).astype(bf16)
            sim_ref[rows, :] = sim
            totals = lax.dot_general(ones, sim, (((1,), (1,)), ((), ())), preferred_element_type=f32)
            for q in range(TILE // LANES):
                total_ref[:, first // LANES + q, :] = totals[:, q * LANES : (q + 1) * LANES]

    in_turn(len(spans), into, work, ahead=3)


def column_kernel(parts_ref, sim_ref, out_ref):
    factor = 1.0 / jnp.sum(parts_ref[...], axis=0)
    lhs = two_terms(as_row(factor))
    sums = jnp.dot(lhs, sim_ref[...], preferred_element_type=f32)
    out_ref[...] = jnp.broadcast_to(as_tiles(jnp.sum(sums, axis=0, keepdims=True))[None], out_ref.shape)


def row_kernel(desired_load, parts_ref, sim_ref, out_ref):
    factor = desired_load / jnp.sum(parts_ref[...], axis=0)
    lhs = two_terms(as_row(factor))
    sums = lax.dot_general(lhs, sim_ref[...], (((1,), (1,)), ((), ())), preferred_element_type=f32)
    out_ref[...] = jnp.broadcast_to(as_tiles(jnp.sum(sums, axis=0, keepdims=True))[None], out_ref.shape)


def down(row):
    return jnp.transpose(jnp.broadcast_to(row, (LANES, LANES)))


def numerator_kernel(count, parts_ref, sim_ref, x_ref, out_ref, weight_ref):
    factor = 1.0 / jnp.sum(parts_ref[...], axis=0)
    lhs = two_terms(as_row(factor))
    mass = jnp.sum(jnp.dot(lhs, sim_ref[...], preferred_element_type=f32), axis=0, keepdims=True)
    columns = sim_ref.shape[1]
    for q in range(sim_ref.shape[0] // LANES):
        rows = pl.ds(q * LANES, LANES)
        scale = jnp.concatenate([down(factor[q : q + 1])] * (columns // LANES), axis=1)
        weight_ref[rows, :] = (sim_ref[rows, :].astype(f32) * scale).astype(bf16)
    chunks = x_ref.shape[1] // LANES
    held = columns // out_ref.shape[0]
    base = held * chunks
    for t in range(columns // TILE):
        sums = lax.dot_general(
            weight_ref[:, pl.ds(t * TILE, TILE)],
            x_ref[...],
            (((0,), (0,)), ((), ())),
            preferred_element_type=f32,
        ).astype(bf16)
        for z in range(TILE // count):
            slot, place = divmod(t * TILE + z * count, held)
            for c in range(chunks):
                out_ref[slot, pl.ds(place * chunks + c * count, count), :] = sums[
                    z * count : (z + 1) * count, c * LANES : (c + 1) * LANES
                ]
    for i in range(out_ref.shape[0]):
        own = as_tiles(mass[:, i * held : (i + 1) * held])
        rest = jnp.zeros((out_ref.shape[1] - base - own.shape[0], LANES), f32)
        out_ref[i, pl.ds(base, out_ref.shape[1] - base), :] = jnp.concatenate([own, rest], axis=0).astype(bf16)


def hand_on_kernel(count, parts_ref, out_ref):
    total = jnp.sum(parts_ref[...].astype(f32), axis=0)
    chunk_rows = out_ref.shape[1] - 8
    base = chunk_rows * out_ref.shape[0]
    for z in range(out_ref.shape[0]):
        out_ref[z, pl.ds(0, chunk_rows), :] = total[z * chunk_rows : (z + 1) * chunk_rows].astype(bf16)
        at = z * count % LANES
        row = total[base + z * count // LANES : base + z * count // LANES + 1]
        row = jnp.concatenate([row[:, at:], row[:, :at]], axis=1) if at else row
        out_ref[z, pl.ds(chunk_rows, 8), :] = jnp.broadcast_to(row, (8, LANES)).astype(bf16)


def update_kernel(parts_ref, cent_ref, out_ref):
    total = jnp.sum(parts_ref[...].astype(f32), axis=0)
    count, width = out_ref.shape
    chunk_rows = width // LANES * count
    scale = 1.0 / (down(total[chunk_rows : chunk_rows + 1])[:count] + 1.0)
    for c in range(width // LANES):
        lanes = pl.ds(c * LANES, LANES)
        out_ref[:, lanes] = (total[c * count : (c + 1) * count] + cent_ref[:, lanes]) * scale


def call(kernel, name, operands, outs, mib, flops, scratch=(), hbm_in=(), hbm_out=False):
    moved = sum(math.prod(o.shape) * o.dtype.itemsize for o in (*operands, *outs))
    vmem, hbm = pl.BlockSpec(memory_space=pltpu.VMEM), pl.BlockSpec(memory_space=pltpu.HBM)
    out = hbm if hbm_out else vmem
    single = len(outs) == 1
    if hbm_out:
        outs = [pltpu.HBM(o.shape, o.dtype) for o in outs]
    operands = [
        pltpu.with_memory_space_constraint(o, pltpu.HBM) if i in hbm_in else o
        for i, o in enumerate(operands)
    ]
    return pl.pallas_call(
        kernel,
        name=name,
        out_shape=outs[0] if single else outs,
        in_specs=[hbm if i in hbm_in else vmem for i in range(len(operands))],
        out_specs=out if single else [out] * len(outs),
        scratch_shapes=scratch,
        compiler_params=pltpu.CompilerParams(vmem_limit_bytes=mib * MIB),
        cost_estimate=pl.CostEstimate(flops=flops, bytes_accessed=moved, transcendentals=0),
    )(*operands)


def per_device(embeddings, coarse_ids, centroids, coarse_of):
    row_count, width = embeddings.shape
    local_count = centroids.shape[0]
    near, far, along_z = ("x", "zl"), "zh", ("zh", "zl")
    x_size, near_size, far_size = (lax.axis_size(axes) for axes in ("x", near, far))
    z_size = lax.axis_size(along_z)
    cent_size = lax.axis_size(("y", "core"))
    columns = x_size * z_size * local_count
    desired_load = row_count / (local_count * cent_size)
    layout_table = coarse_of.reshape(x_size, far_size, z_size // far_size, cent_size, local_count)
    group_ids = lax.dynamic_index_in_dim(
        layout_table, lax.axis_index(("y", "core")), 3, keepdims=False
    )
    group_ids = jnp.swapaxes(group_ids, 1, 2).reshape(1, columns)

    array = jax.ShapeDtypeStruct
    unit_like, match_like = array((row_count, width), bf16), array((row_count, columns), bf16)
    blocks = row_count // TILE
    unit_x, matched = call(
        prepare_kernel,
        "prepare",
        (embeddings, coarse_ids, group_ids),
        (unit_like, match_like),
        24,
        8 * row_count * CLUSTERS * columns,
        scratch=[
            pltpu.VMEM(unit_like.shape, bf16),
            pltpu.VMEM(unit_like.shape, bf16),
            pltpu.VMEM(match_like.shape, bf16),
            pltpu.VMEM((CLUSTERS, columns), bf16),
            pltpu.SemaphoreType.DMA((3, blocks)),
        ],
        hbm_in=(0,),
        hbm_out=True,
    )
    copies = call(
        unit_copies_kernel, "units", (centroids,), (array((far_size, local_count, width), bf16),), 4, 0
    )
    part = exchange(copies, far)
    copies = call(copies_kernel, "copies", (part,), (array((near_size,) + part.shape, bf16),), 4, 0)
    group_centroids = exchange(copies, near).reshape(columns, width)

    product = 2 * row_count * columns
    row_parts = array((cent_size, row_count // LANES, LANES), f32)
    column_parts = array((x_size, columns // LANES, LANES), f32)
    column_sums = array((z_size, columns // LANES, LANES), f32)
    similarity, parts = call(
        similarity_kernel,
        "similarity",
        (unit_x, group_centroids, matched),
        (match_like, row_parts),
        20,
        product * width,
        scratch=[
            pltpu.VMEM(unit_like.shape, bf16),
            pltpu.VMEM(match_like.shape, bf16),
            pltpu.SemaphoreType.DMA((2, blocks)),
        ],
        hbm_in=(0, 2),
    )
    parts = exchange(parts, ("y", "core"))
    for sweep in range(SWEEPS):
        parts = call(column_kernel, "columns", (parts, similarity), (column_parts,), 8, product * 16)
        parts = call(sum_copies_kernel, "across", (exchange(parts, "x"),), (column_sums,), 2, 0)
        parts = call(
            functools.partial(row_kernel, desired_load),
            "rows",
            (exchange(parts, along_z), similarity),
            (row_parts,),
            8,
            product * 16,
        )
        parts = exchange(parts, ("y", "core"))
    chunk_rows = width // LANES * local_count
    sums = call(
        functools.partial(numerator_kernel, local_count),
        "numerator",
        (parts, similarity, embeddings),
        (array((near_size, far_size * chunk_rows + 16, LANES), bf16),),
        16,
        product * width,
        scratch=[pltpu.VMEM((row_count, columns), bf16)],
    )
    sums = call(
        functools.partial(hand_on_kernel, local_count),
        "hand_on",
        (exchange(sums, near),),
        (array((far_size, chunk_rows + 8, LANES), bf16),),
        8,
        0,
    )
    return call(
        update_kernel,
        "update",
        (exchange(sums, far), centroids),
        (array(centroids.shape, f32),),
        4,
        0,
    )


def solution(mesh):
    fine = Mesh(mesh.devices.reshape(4, 8, 2, 4, 2), ("x", "zh", "zl", "y", "core"))
    rows, held = P(("x", "zh", "zl"), None), P(("x", "zh", "zl", "y", "core"), None)
    return jax.shard_map(
        per_device,
        mesh=fine,
        in_specs=(rows, rows, held, P()),
        out_specs=held,
        check_vma=False,
    )
```

```python
import functools
import math

import jax
import jax.numpy as jnp
from jax import lax
from jax.experimental import pallas as pl
from jax.experimental.pallas import tpu as pltpu
from jax.sharding import Mesh
from jax.sharding import PartitionSpec as P

SWEEPS = 3
CLUSTERS = 512
LANES = 128
TILE = 256


entropic_smoothing = 0.03
MIB = 1 << 20
f32, bf16 = jnp.float32, jnp.bfloat16


def unit_rows(values):
    values = values.astype(f32)
    return values * lax.rsqrt(jnp.sum(values * values, axis=-1, keepdims=True) + 1e-06)


def exchange(blocks, axes):
    return lax.all_to_all(blocks, axes, 0, 0)


def as_row(tiles):
    return jnp.concatenate([tiles[q : q + 1] for q in range(tiles.shape[0])], axis=1)


def as_tiles(row):
    count = row.shape[1] // LANES
    return jnp.concatenate([row[:, q * LANES : (q + 1) * LANES] for q in range(count)], axis=0)


def two_terms(row):
    wide = jnp.broadcast_to(row, (16, row.shape[1]))
    high = wide.astype(bf16).astype(f32)
    which = lax.broadcasted_iota(jnp.int32, wide.shape, 0)
    rest = jnp.where(which == 1, wide - high, 0.0)
    return jnp.where(which == 0, high, rest).astype(bf16)


def in_turn(blocks, copies, work, ahead=2):
    for b in range(min(ahead, blocks)):
        for copy in copies(b):
            copy.start()
    for b in range(blocks):
        if b + ahead < blocks:
            for copy in copies(b + ahead):
                copy.start()
        for copy in copies(b):
            copy.wait()
        work(b)


def prepare_kernel(x_hbm, ids_ref, group_ref, unit_hbm, match_hbm, x_ref, unit_ref, match_ref, hot_ref, sems):
    blocks = x_ref.shape[0] // TILE
    half = CLUSTERS // 2
    cluster = lax.broadcasted_iota(jnp.int32, hot_ref.shape, 0)
    hot_ref[...] = jnp.where(cluster == group_ref[...], 1.0, 0.0).astype(bf16)
    lane = lax.broadcasted_iota(jnp.int32, (TILE, half), 1).astype(f32).astype(bf16)

    def into(b):
        rows = pl.ds(b * TILE, TILE)
        return (pltpu.make_async_copy(x_hbm.at[rows], x_ref.at[rows], sems.at[0, b]),)

    def out_of(b):
        rows = pl.ds(b * TILE, TILE)
        return (
            pltpu.make_async_copy(unit_ref.at[rows], unit_hbm.at[rows], sems.at[1, b]),
            pltpu.make_async_copy(match_ref.at[rows], match_hbm.at[rows], sems.at[2, b]),
        )

    def work(b):
        rows = pl.ds(b * TILE, TILE)
        unit_ref[rows, :] = unit_rows(x_ref[rows, :]).astype(bf16)
        ids = ids_ref[rows, :]
        matched = jnp.zeros((TILE, match_ref.shape[1]), f32)
        for first in (0, half):
            near = (ids - first).astype(f32).astype(bf16)
            picked = jnp.zeros(lane.shape, bf16)
            for p in range(ids.shape[1]):
                picked = jnp.where(near[:, p : p + 1] == lane, jnp.ones_like(picked), picked)
            matched += jnp.dot(picked, hot_ref[first : first + half, :], preferred_element_type=f32)
        match_ref[rows, :] = matched.astype(bf16)
        for copy in out_of(b):
            copy.start()

    in_turn(blocks, into, work)
    for b in range(blocks):
        for copy in out_of(b):
            copy.wait()


def unit_copies_kernel(cent_ref, out_ref):
    out_ref[...] = jnp.broadcast_to(unit_rows(cent_ref[...]).astype(bf16)[None], out_ref.shape)


def copies_kernel(block_ref, out_hbm, sems):
    copies = [
        pltpu.make_async_copy(block_ref, out_hbm.at[i], sems.at[i]) for i in range(out_hbm.shape[0])
    ]
    for copy in copies:
        copy.start()
    for copy in copies:
        copy.wait()


def sum_copies_kernel(parts_ref, out_ref):
    out_ref[...] = jnp.broadcast_to(jnp.sum(parts_ref[...], axis=0)[None], out_ref.shape)


def similarity_kernel(unit_hbm, cent_ref, match_hbm, sim_ref, total_ref, unit_ref, match_ref, sems):
    ones = jnp.ones((total_ref.shape[0], sim_ref.shape[1]), bf16)
    scale = math.log2(math.e) / entropic_smoothing
    total_rows = unit_ref.shape[0]
    starts = [0, LANES, TILE] + list(range(2 * TILE, total_rows, 2 * TILE))
    spans = [pl.ds(i, j - i) for i, j in zip(starts, starts[1:] + [total_rows])]

    def into(b):
        rows = spans[b]
        return (
            pltpu.make_async_copy(unit_hbm.at[rows], unit_ref.at[rows], sems.at[0, b]),
            pltpu.make_async_copy(match_hbm.at[rows], match_ref.at[rows], sems.at[1, b]),
        )

    def work(b):
        step = min(TILE, spans[b].size)
        for first in range(starts[b], starts[b] + spans[b].size, step):
            rows = pl.ds(first, step)
            dots = lax.dot_general(
                unit_ref[rows, :], cent_ref[...], (((1,), (1,)), ((), ())), preferred_element_type=f32
            )
            sim = (jnp.exp2(dots * scale) * match_ref[rows, :].astype(f32)).astype(bf16)
            sim_ref[rows, :] = sim
            totals = lax.dot_general(ones, sim, (((1,), (1,)), ((), ())), preferred_element_type=f32)
            for q in range(step // LANES):
                total_ref[:, first // LANES + q, :] = totals[:, q * LANES : (q + 1) * LANES]

    in_turn(len(spans), into, work)


def column_kernel(parts_ref, sim_ref, out_ref):
    factor = 1.0 / jnp.sum(parts_ref[...], axis=0)
    lhs = two_terms(as_row(factor))
    sums = jnp.dot(lhs, sim_ref[...], preferred_element_type=f32)
    out_ref[...] = jnp.broadcast_to(as_tiles(jnp.sum(sums, axis=0, keepdims=True))[None], out_ref.shape)


def row_kernel(desired_load, parts_ref, sim_ref, out_ref):
    factor = desired_load / jnp.sum(parts_ref[...], axis=0)
    lhs = two_terms(as_row(factor))
    sums = lax.dot_general(lhs, sim_ref[...], (((1,), (1,)), ((), ())), preferred_element_type=f32)
    out_ref[...] = jnp.broadcast_to(as_tiles(jnp.sum(sums, axis=0, keepdims=True))[None], out_ref.shape)


def down(row):
    return jnp.transpose(jnp.broadcast_to(row, (LANES, LANES)))


def numerator_kernel(count, parts_ref, sim_ref, x_ref, out_ref, weight_ref):
    factor = 1.0 / jnp.sum(parts_ref[...], axis=0)
    lhs = two_terms(as_row(factor))
    mass = jnp.sum(jnp.dot(lhs, sim_ref[...], preferred_element_type=f32), axis=0, keepdims=True)
    columns = sim_ref.shape[1]
    for q in range(sim_ref.shape[0] // LANES):
        rows = pl.ds(q * LANES, LANES)
        scale = jnp.concatenate([down(factor[q : q + 1])] * (columns // LANES), axis=1)
        weight_ref[rows, :] = (sim_ref[rows, :].astype(f32) * scale).astype(bf16)
    chunks = x_ref.shape[1] // LANES
    held = columns // out_ref.shape[0]
    base = held * chunks
    for t in range(columns // TILE):
        sums = lax.dot_general(
            weight_ref[:, pl.ds(t * TILE, TILE)],
            x_ref[...],
            (((0,), (0,)), ((), ())),
            preferred_element_type=f32,
        ).astype(bf16)
        for z in range(TILE // count):
            slot, place = divmod(t * TILE + z * count, held)
            for c in range(chunks):
                out_ref[slot, pl.ds(place * chunks + c * count, count), :] = sums[
                    z * count : (z + 1) * count, c * LANES : (c + 1) * LANES
                ]
    for i in range(out_ref.shape[0]):
        own = as_tiles(mass[:, i * held : (i + 1) * held])
        rest = jnp.zeros((out_ref.shape[1] - base - own.shape[0], LANES), f32)
        out_ref[i, pl.ds(base, out_ref.shape[1] - base), :] = jnp.concatenate([own, rest], axis=0).astype(bf16)


def hand_on_kernel(count, parts_ref, out_ref):
    total = jnp.sum(parts_ref[...].astype(f32), axis=0)
    chunk_rows = out_ref.shape[1] - 8
    base = chunk_rows * out_ref.shape[0]
    for z in range(out_ref.shape[0]):
        out_ref[z, pl.ds(0, chunk_rows), :] = total[z * chunk_rows : (z + 1) * chunk_rows].astype(bf16)
        at = z * count % LANES
        row = total[base + z * count // LANES : base + z * count // LANES + 1]
        row = jnp.concatenate([row[:, at:], row[:, :at]], axis=1) if at else row
        out_ref[z, pl.ds(chunk_rows, 8), :] = jnp.broadcast_to(row, (8, LANES)).astype(bf16)


def update_kernel(parts_ref, cent_ref, out_ref):
    total = jnp.sum(parts_ref[...].astype(f32), axis=0)
    count, width = out_ref.shape
    chunk_rows = width // LANES * count
    scale = 1.0 / (down(total[chunk_rows : chunk_rows + 1])[:count] + 1.0)
    for c in range(width // LANES):
        lanes = pl.ds(c * LANES, LANES)
        out_ref[:, lanes] = (total[c * count : (c + 1) * count] + cent_ref[:, lanes]) * scale


def call(kernel, name, operands, outs, mib, flops, scratch=(), hbm_in=(), hbm_out=False):
    moved = sum(math.prod(o.shape) * o.dtype.itemsize for o in (*operands, *outs))
    vmem, hbm = pl.BlockSpec(memory_space=pltpu.VMEM), pl.BlockSpec(memory_space=pltpu.HBM)
    out = hbm if hbm_out else vmem
    single = len(outs) == 1
    if hbm_out:
        outs = tuple(pltpu.HBM(o.shape, o.dtype) for o in outs)
    operands = [
        pltpu.with_memory_space_constraint(o, pltpu.HBM) if i in hbm_in else o
        for i, o in enumerate(operands)
    ]
    return pl.pallas_call(
        kernel,
        name=name,
        out_shape=outs[0] if single else outs,
        in_specs=[hbm if i in hbm_in else vmem for i in range(len(operands))],
        out_specs=out if single else [out] * len(outs),
        scratch_shapes=scratch,
        compiler_params=pltpu.CompilerParams(vmem_limit_bytes=mib * MIB),
        cost_estimate=pl.CostEstimate(flops=flops, bytes_accessed=moved, transcendentals=0),
    )(*operands)


def per_device(embeddings, coarse_ids, centroids, coarse_of):
    row_count, width = embeddings.shape
    local_count = centroids.shape[0]
    near, far, along_z = ("x", "zl"), "zh", ("zh", "zl")
    x_size, near_size, far_size = (lax.axis_size(axes) for axes in ("x", near, far))
    z_size = lax.axis_size(along_z)
    cent_size = lax.axis_size(("y", "core"))
    columns = x_size * z_size * local_count
    desired_load = row_count / (local_count * cent_size)
    layout_table = coarse_of.reshape(x_size, far_size, z_size // far_size, cent_size, local_count)
    group_ids = lax.dynamic_index_in_dim(
        layout_table, lax.axis_index(("y", "core")), 3, keepdims=False
    )
    group_ids = jnp.swapaxes(group_ids, 1, 2).reshape(1, columns)

    array = jax.ShapeDtypeStruct
    unit_like, match_like = array((row_count, width), bf16), array((row_count, columns), bf16)
    blocks = row_count // TILE
    unit_x, matched = call(
        prepare_kernel,
        "prepare",
        (embeddings, coarse_ids, group_ids),
        (unit_like, match_like),
        24,
        8 * row_count * CLUSTERS * columns,
        scratch=[
            pltpu.VMEM(unit_like.shape, bf16),
            pltpu.VMEM(unit_like.shape, bf16),
            pltpu.VMEM(match_like.shape, bf16),
            pltpu.VMEM((CLUSTERS, columns), bf16),
            pltpu.SemaphoreType.DMA((3, blocks)),
        ],
        hbm_in=(0,),
        hbm_out=True,
    )
    copies = call(
        unit_copies_kernel, "units", (centroids,), (array((far_size, local_count, width), bf16),), 4, 0
    )
    part = exchange(copies, far)
    copies = call(
        copies_kernel,
        "copies",
        (part,),
        (array((near_size,) + part.shape, bf16),),
        4,
        0,
        scratch=[pltpu.SemaphoreType.DMA((near_size,))],
        hbm_out=True,
    )
    group_centroids = exchange(copies, near).reshape(columns, width)

    product = 2 * row_count * columns
    row_parts = array((cent_size, row_count // LANES, LANES), f32)
    column_parts = array((x_size, columns // LANES, LANES), f32)
    column_sums = array((z_size, columns // LANES, LANES), f32)
    similarity, parts = call(
        similarity_kernel,
        "similarity",
        (unit_x, group_centroids, matched),
        (match_like, row_parts),
        20,
        product * width,
        scratch=[
            pltpu.VMEM(unit_like.shape, bf16),
            pltpu.VMEM(match_like.shape, bf16),
            pltpu.SemaphoreType.DMA((2, blocks)),
        ],
        hbm_in=(0, 2),
    )
    parts = exchange(parts, ("y", "core"))
    for sweep in range(SWEEPS):
        parts = call(column_kernel, "columns", (parts, similarity), (column_parts,), 8, product * 16)
        parts = call(sum_copies_kernel, "across", (exchange(parts, "x"),), (column_sums,), 2, 0)
        parts = call(
            functools.partial(row_kernel, desired_load),
            "rows",
            (exchange(parts, along_z), similarity),
            (row_parts,),
            8,
            product * 16,
        )
        parts = exchange(parts, ("y", "core"))
    chunk_rows = width // LANES * local_count
    sums = call(
        functools.partial(numerator_kernel, local_count),
        "numerator",
        (parts, similarity, embeddings),
        (array((near_size, far_size * chunk_rows + 16, LANES), bf16),),
        16,
        product * width,
        scratch=[pltpu.VMEM((row_count, columns), bf16)],
    )
    sums = call(
        functools.partial(hand_on_kernel, local_count),
        "hand_on",
        (exchange(sums, near),),
        (array((far_size, chunk_rows + 8, LANES), bf16),),
        8,
        0,
    )
    return call(
        update_kernel,
        "update",
        (exchange(sums, far), centroids),
        (array(centroids.shape, f32),),
        4,
        0,
    )


def solution(mesh):
    fine = Mesh(mesh.devices.reshape(4, 8, 2, 4, 2), ("x", "zh", "zl", "y", "core"))
    rows, held = P(("x", "zh", "zl"), None), P(("x", "zh", "zl", "y", "core"), None)
    return jax.shard_map(
        per_device,
        mesh=fine,
        in_specs=(rows, rows, held, P()),
        out_specs=held,
        check_vma=False,
    )
```

```python
import functools
import math

import jax
import jax.numpy as jnp
from jax import lax
from jax.experimental import pallas as pl
from jax.experimental.pallas import tpu as pltpu
from jax.sharding import Mesh
from jax.sharding import PartitionSpec as P

SWEEPS = 3
CLUSTERS = 512
LANES = 128
TILE = 256


entropic_smoothing = 0.03
MIB = 1 << 20
f32, bf16 = jnp.float32, jnp.bfloat16


def unit_rows(values):
    values = values.astype(f32)
    return values * lax.rsqrt(jnp.sum(values * values, axis=-1, keepdims=True) + 1e-06)


def exchange(blocks, axes):
    return lax.all_to_all(blocks, axes, 0, 0)


def as_row(tiles):
    return jnp.concatenate([tiles[q : q + 1] for q in range(tiles.shape[0])], axis=1)


def as_tiles(row):
    count = row.shape[1] // LANES
    return jnp.concatenate([row[:, q * LANES : (q + 1) * LANES] for q in range(count)], axis=0)


def two_terms(row):
    wide = jnp.broadcast_to(row, (16, row.shape[1]))
    high = wide.astype(bf16).astype(f32)
    which = lax.broadcasted_iota(jnp.int32, wide.shape, 0)
    rest = jnp.where(which == 1, wide - high, 0.0)
    return jnp.where(which == 0, high, rest).astype(bf16)


def in_turn(blocks, copies, work, ahead=2):
    for b in range(min(ahead, blocks)):
        for copy in copies(b):
            copy.start()
    for b in range(blocks):
        if b + ahead < blocks:
            for copy in copies(b + ahead):
                copy.start()
        for copy in copies(b):
            copy.wait()
        work(b)


def prepare_kernel(x_hbm, ids_ref, group_ref, unit_hbm, match_hbm, x_ref, unit_ref, match_ref, hot_ref, sems):
    blocks = x_ref.shape[0] // TILE
    half = CLUSTERS // 2
    cluster = lax.broadcasted_iota(jnp.int32, hot_ref.shape, 0)
    hot_ref[...] = jnp.where(cluster == group_ref[...], 1.0, 0.0).astype(bf16)
    lane = lax.broadcasted_iota(jnp.int32, (TILE, half), 1).astype(f32).astype(bf16)

    def into(b):
        rows = pl.ds(b * TILE, TILE)
        return (pltpu.make_async_copy(x_hbm.at[rows], x_ref.at[rows], sems.at[0, b]),)

    def out_of(b):
        rows = pl.ds(b * TILE, TILE)
        return (
            pltpu.make_async_copy(unit_ref.at[rows], unit_hbm.at[rows], sems.at[1, b]),
            pltpu.make_async_copy(match_ref.at[rows], match_hbm.at[rows], sems.at[2, b]),
        )

    def work(b):
        rows = pl.ds(b * TILE, TILE)
        unit_ref[rows, :] = unit_rows(x_ref[rows, :]).astype(bf16)
        ids = ids_ref[rows, :]
        matched = jnp.zeros((TILE, match_ref.shape[1]), f32)
        for first in (0, half):
            near = (ids - first).astype(f32).astype(bf16)
            picked = jnp.zeros(lane.shape, bf16)
            for p in range(ids.shape[1]):
                picked = jnp.where(near[:, p : p + 1] == lane, jnp.ones_like(picked), picked)
            matched += jnp.dot(picked, hot_ref[first : first + half, :], preferred_element_type=f32)
        match_ref[rows, :] = matched.astype(bf16)
        for copy in out_of(b):
            copy.start()

    in_turn(blocks, into, work)
    for b in range(blocks):
        for copy in out_of(b):
            copy.wait()


def unit_copies_kernel(cent_ref, out_ref):
    out_ref[...] = jnp.broadcast_to(unit_rows(cent_ref[...]).astype(bf16)[None], out_ref.shape)


def copies_kernel(block_ref, out_ref):
    for i in range(out_ref.shape[0]):
        out_ref[i] = block_ref[...]


def sum_copies_kernel(parts_ref, out_ref):
    out_ref[...] = jnp.broadcast_to(jnp.sum(parts_ref[...], axis=0)[None], out_ref.shape)


def similarity_kernel(unit_hbm, cent_ref, match_hbm, sim_ref, total_ref, unit_ref, match_ref, sems):
    ones = jnp.ones((total_ref.shape[0], sim_ref.shape[1]), bf16)
    scale = math.log2(math.e) / entropic_smoothing
    total_rows = unit_ref.shape[0]
    starts = [0, total_rows // 4]
    spans = [pl.ds(i, j - i) for i, j in zip(starts, starts[1:] + [total_rows])]

    def into(b):
        rows = spans[b]
        return (
            pltpu.make_async_copy(unit_hbm.at[rows], unit_ref.at[rows], sems.at[0, b]),
            pltpu.make_async_copy(match_hbm.at[rows], match_ref.at[rows], sems.at[1, b]),
        )

    def work(b):
        for first in range(starts[b], starts[b] + spans[b].size, TILE):
            rows = pl.ds(first, TILE)
            dots = lax.dot_general(
                unit_ref[rows, :], cent_ref[...], (((1,), (1,)), ((), ())), preferred_element_type=f32
            )
            sim = (jnp.exp2(dots * scale) * match_ref[rows, :].astype(f32)).astype(bf16)
            sim_ref[rows, :] = sim
            totals = lax.dot_general(ones, sim, (((1,), (1,)), ((), ())), preferred_element_type=f32)
            for q in range(TILE // LANES):
                total_ref[:, first // LANES + q, :] = totals[:, q * LANES : (q + 1) * LANES]

    in_turn(len(spans), into, work)


def column_kernel(parts_ref, sim_ref, out_ref):
    factor = 1.0 / jnp.sum(parts_ref[...], axis=0)
    lhs = two_terms(as_row(factor))
    sums = jnp.dot(lhs, sim_ref[...], preferred_element_type=f32)
    out_ref[...] = jnp.broadcast_to(as_tiles(jnp.sum(sums, axis=0, keepdims=True))[None], out_ref.shape)


def row_kernel(desired_load, parts_ref, sim_ref, out_ref):
    factor = desired_load / jnp.sum(parts_ref[...], axis=0)
    lhs = two_terms(as_row(factor))
    sums = lax.dot_general(lhs, sim_ref[...], (((1,), (1,)), ((), ())), preferred_element_type=f32)
    out_ref[...] = jnp.broadcast_to(as_tiles(jnp.sum(sums, axis=0, keepdims=True))[None], out_ref.shape)


def down(row):
    return jnp.transpose(jnp.broadcast_to(row, (LANES, LANES)))


def numerator_kernel(count, parts_ref, sim_ref, x_ref, out_ref, weight_ref):
    factor = 1.0 / jnp.sum(parts_ref[...], axis=0)
    lhs = two_terms(as_row(factor))
    mass = jnp.sum(jnp.dot(lhs, sim_ref[...], preferred_element_type=f32), axis=0, keepdims=True)
    columns = sim_ref.shape[1]
    for q in range(sim_ref.shape[0] // LANES):
        rows = pl.ds(q * LANES, LANES)
        scale = jnp.concatenate([down(factor[q : q + 1])] * (columns // LANES), axis=1)
        weight_ref[rows, :] = (sim_ref[rows, :].astype(f32) * scale).astype(bf16)
    chunks = x_ref.shape[1] // LANES
    held = columns // out_ref.shape[0]
    base = held * chunks
    for t in range(columns // TILE):
        sums = lax.dot_general(
            weight_ref[:, pl.ds(t * TILE, TILE)],
            x_ref[...],
            (((0,), (0,)), ((), ())),
            preferred_element_type=f32,
        ).astype(bf16)
        for z in range(TILE // count):
            slot, place = divmod(t * TILE + z * count, held)
            for c in range(chunks):
                out_ref[slot, pl.ds(place * chunks + c * count, count), :] = sums[
                    z * count : (z + 1) * count, c * LANES : (c + 1) * LANES
                ]
    for i in range(out_ref.shape[0]):
        own = as_tiles(mass[:, i * held : (i + 1) * held])
        rest = jnp.zeros((out_ref.shape[1] - base - own.shape[0], LANES), f32)
        out_ref[i, pl.ds(base, out_ref.shape[1] - base), :] = jnp.concatenate([own, rest], axis=0).astype(bf16)


def hand_on_kernel(count, parts_ref, out_ref):
    total = jnp.sum(parts_ref[...].astype(f32), axis=0)
    chunk_rows = out_ref.shape[1] - 8
    base = chunk_rows * out_ref.shape[0]
    for z in range(out_ref.shape[0]):
        out_ref[z, pl.ds(0, chunk_rows), :] = total[z * chunk_rows : (z + 1) * chunk_rows].astype(bf16)
        at = z * count % LANES
        row = total[base + z * count // LANES : base + z * count // LANES + 1]
        row = jnp.concatenate([row[:, at:], row[:, :at]], axis=1) if at else row
        out_ref[z, pl.ds(chunk_rows, 8), :] = jnp.broadcast_to(row, (8, LANES)).astype(bf16)


def update_kernel(parts_ref, cent_ref, out_ref):
    total = jnp.sum(parts_ref[...].astype(f32), axis=0)
    count, width = out_ref.shape
    chunk_rows = width // LANES * count
    scale = 1.0 / (down(total[chunk_rows : chunk_rows + 1])[:count] + 1.0)
    for c in range(width // LANES):
        lanes = pl.ds(c * LANES, LANES)
        out_ref[:, lanes] = (total[c * count : (c + 1) * count] + cent_ref[:, lanes]) * scale


def call(kernel, name, operands, outs, mib, flops, scratch=(), hbm_in=(), hbm_out=False):
    moved = sum(math.prod(o.shape) * o.dtype.itemsize for o in (*operands, *outs))
    vmem, hbm = pl.BlockSpec(memory_space=pltpu.VMEM), pl.BlockSpec(memory_space=pltpu.HBM)
    out = hbm if hbm_out else vmem
    single = len(outs) == 1
    if hbm_out:
        outs = [pltpu.HBM(o.shape, o.dtype) for o in outs]
    operands = [
        pltpu.with_memory_space_constraint(o, pltpu.HBM) if i in hbm_in else o
        for i, o in enumerate(operands)
    ]
    return pl.pallas_call(
        kernel,
        name=name,
        out_shape=outs[0] if single else outs,
        in_specs=[hbm if i in hbm_in else vmem for i in range(len(operands))],
        out_specs=out if single else [out] * len(outs),
        scratch_shapes=scratch,
        compiler_params=pltpu.CompilerParams(vmem_limit_bytes=mib * MIB),
        cost_estimate=pl.CostEstimate(flops=flops, bytes_accessed=moved, transcendentals=0),
    )(*operands)


def per_device(embeddings, coarse_ids, centroids, coarse_of):
    row_count, width = embeddings.shape
    local_count = centroids.shape[0]
    near, far, along_z = ("x", "zl"), "zh", ("zh", "zl")
    x_size, near_size, far_size = (lax.axis_size(axes) for axes in ("x", near, far))
    z_size = lax.axis_size(along_z)
    cent_size = lax.axis_size(("y", "core"))
    columns = x_size * z_size * local_count
    desired_load = row_count / (local_count * cent_size)
    layout_table = coarse_of.reshape(x_size, far_size, z_size // far_size, cent_size, local_count)
    group_ids = lax.dynamic_index_in_dim(
        layout_table, lax.axis_index(("y", "core")), 3, keepdims=False
    )
    group_ids = jnp.swapaxes(group_ids, 1, 2).reshape(1, columns)

    array = jax.ShapeDtypeStruct
    unit_like, match_like = array((row_count, width), bf16), array((row_count, columns), bf16)
    blocks = row_count // TILE
    unit_x, matched = call(
        prepare_kernel,
        "prepare",
        (embeddings, coarse_ids, group_ids),
        (unit_like, match_like),
        24,
        8 * row_count * CLUSTERS * columns,
        scratch=[
            pltpu.VMEM(unit_like.shape, bf16),
            pltpu.VMEM(unit_like.shape, bf16),
            pltpu.VMEM(match_like.shape, bf16),
            pltpu.VMEM((CLUSTERS, columns), bf16),
            pltpu.SemaphoreType.DMA((3, blocks)),
        ],
        hbm_in=(0,),
        hbm_out=True,
    )
    copies = call(
        unit_copies_kernel, "units", (centroids,), (array((far_size, local_count, width), bf16),), 4, 0
    )
    part = exchange(copies, far)
    copies = call(copies_kernel, "copies", (part,), (array((near_size,) + part.shape, bf16),), 4, 0)
    group_centroids = exchange(copies, near).reshape(columns, width)

    product = 2 * row_count * columns
    row_parts = array((cent_size, row_count // LANES, LANES), f32)
    column_parts = array((x_size, columns // LANES, LANES), f32)
    column_sums = array((z_size, columns // LANES, LANES), f32)
    similarity, parts = call(
        similarity_kernel,
        "similarity",
        (unit_x, group_centroids, matched),
        (match_like, row_parts),
        20,
        product * width,
        scratch=[
            pltpu.VMEM(unit_like.shape, bf16),
            pltpu.VMEM(match_like.shape, bf16),
            pltpu.SemaphoreType.DMA((2, blocks)),
        ],
        hbm_in=(0, 2),
    )
    parts = exchange(parts, ("y", "core"))
    for sweep in range(SWEEPS):
        parts = call(column_kernel, "columns", (parts, similarity), (column_parts,), 8, product * 16)
        parts = call(sum_copies_kernel, "across", (exchange(parts, "x"),), (column_sums,), 2, 0)
        parts = call(
            functools.partial(row_kernel, desired_load),
            "rows",
            (exchange(parts, along_z), similarity),
            (row_parts,),
            8,
            product * 16,
        )
        parts = exchange(parts, ("y", "core"))
    chunk_rows = width // LANES * local_count
    sums = call(
        functools.partial(numerator_kernel, local_count),
        "numerator",
        (parts, similarity, embeddings),
        (array((near_size, far_size * chunk_rows + 16, LANES), bf16),),
        16,
        product * width,
        scratch=[pltpu.VMEM((row_count, columns), bf16)],
    )
    sums = call(
        functools.partial(hand_on_kernel, local_count),
        "hand_on",
        (exchange(sums, near),),
        (array((far_size, chunk_rows + 8, LANES), bf16),),
        8,
        0,
    )
    return call(
        update_kernel,
        "update",
        (exchange(sums, far), centroids),
        (array(centroids.shape, f32),),
        4,
        0,
    )


def solution(mesh):
    fine = Mesh(mesh.devices.reshape(4, 8, 2, 4, 2), ("x", "zh", "zl", "y", "core"))
    rows, held = P(("x", "zh", "zl"), None), P(("x", "zh", "zl", "y", "core"), None)
    return jax.shard_map(
        per_device,
        mesh=fine,
        in_specs=(rows, rows, held, P()),
        out_specs=held,
        check_vma=False,
    )
```

```python
import functools
import math

import jax
import jax.numpy as jnp
from jax import lax
from jax.experimental import pallas as pl
from jax.experimental.pallas import tpu as pltpu
from jax.sharding import Mesh
from jax.sharding import PartitionSpec as P

SWEEPS = 3
CLUSTERS = 512
LANES = 128
TILE = 256


entropic_smoothing = 0.03
MIB = 1 << 20
f32, bf16 = jnp.float32, jnp.bfloat16


def unit_rows(values):
    values = values.astype(f32)
    return values * lax.rsqrt(jnp.sum(values * values, axis=-1, keepdims=True) + 1e-06)


def exchange(blocks, axes):
    return lax.all_to_all(blocks, axes, 0, 0)


def as_row(tiles):
    return jnp.concatenate([tiles[q : q + 1] for q in range(tiles.shape[0])], axis=1)


def as_tiles(row):
    count = row.shape[1] // LANES
    return jnp.concatenate([row[:, q * LANES : (q + 1) * LANES] for q in range(count)], axis=0)


def two_terms(row):
    wide = jnp.broadcast_to(row, (16, row.shape[1]))
    high = wide.astype(bf16).astype(f32)
    which = lax.broadcasted_iota(jnp.int32, wide.shape, 0)
    rest = jnp.where(which == 1, wide - high, 0.0)
    return jnp.where(which == 0, high, rest).astype(bf16)


def in_turn(blocks, copies, work, ahead=2):
    for b in range(min(ahead, blocks)):
        for copy in copies(b):
            copy.start()
    for b in range(blocks):
        if b + ahead < blocks:
            for copy in copies(b + ahead):
                copy.start()
        for copy in copies(b):
            copy.wait()
        work(b)


def prepare_kernel(x_hbm, ids_ref, group_ref, unit_hbm, match_hbm, x_ref, unit_ref, match_ref, hot_ref, sems):
    blocks = x_ref.shape[0] // TILE
    half = CLUSTERS // 2
    cluster = lax.broadcasted_iota(jnp.int32, hot_ref.shape, 0)
    hot_ref[...] = jnp.where(cluster == group_ref[...], 1.0, 0.0).astype(bf16)
    which = lax.broadcasted_iota(jnp.int32, (half, TILE), 0).astype(f32).astype(bf16)
    which = which.reshape(half // 16, 16, TILE)

    def into(b):
        rows = pl.ds(b * TILE, TILE)
        return (pltpu.make_async_copy(x_hbm.at[rows], x_ref.at[rows], sems.at[0, b]),)

    def out_of(b):
        rows = pl.ds(b * TILE, TILE)
        return (
            pltpu.make_async_copy(unit_ref.at[rows], unit_hbm.at[rows], sems.at[1, b]),
            pltpu.make_async_copy(match_ref.at[rows], match_hbm.at[rows], sems.at[2, b]),
        )

    def work(b):
        rows = pl.ds(b * TILE, TILE)
        unit_ref[rows, :] = unit_rows(x_ref[rows, :]).astype(bf16)
        ids = ids_ref[:, rows]
        matched = jnp.zeros((TILE, match_ref.shape[1]), f32)
        for first in (0, half):
            near = (ids - first).astype(f32)
            picked = jnp.zeros(which.shape, bf16)
            for p in range(ids.shape[0]):
                pick = jnp.broadcast_to(near[p : p + 1], (16, TILE)).astype(bf16)[None]
                picked = jnp.where(pick == which, jnp.ones_like(picked), picked)
            matched += lax.dot_general(
                picked.reshape(half, TILE),
                hot_ref[first : first + half, :],
                (((0,), (0,)), ((), ())),
                preferred_element_type=f32,
            )
        match_ref[rows, :] = matched.astype(bf16)
        for copy in out_of(b):
            copy.start()

    in_turn(blocks, into, work)
    for b in range(blocks):
        for copy in out_of(b):
            copy.wait()


def unit_copies_kernel(cent_ref, out_ref):
    out_ref[...] = jnp.broadcast_to(unit_rows(cent_ref[...]).astype(bf16)[None], out_ref.shape)


def copies_kernel(block_ref, unused, out_ref):
    for i in range(out_ref.shape[0]):
        out_ref[i] = block_ref[...]


def sum_copies_kernel(parts_ref, out_ref):
    out_ref[...] = jnp.broadcast_to(jnp.sum(parts_ref[...], axis=0)[None], out_ref.shape)


def similarity_kernel(unit_ref, cent_ref, match_ref, sim_ref, total_ref):
    ones = jnp.ones((total_ref.shape[0], sim_ref.shape[1]), bf16)
    scale = math.log2(math.e) / entropic_smoothing
    for b in range(unit_ref.shape[0] // TILE):
        rows = pl.ds(b * TILE, TILE)
        dots = lax.dot_general(
            unit_ref[rows, :], cent_ref[...], (((1,), (1,)), ((), ())), preferred_element_type=f32
        )
        sim = (jnp.exp2(dots * scale) * match_ref[rows, :].astype(f32)).astype(bf16)
        sim_ref[rows, :] = sim
        totals = lax.dot_general(ones, sim, (((1,), (1,)), ((), ())), preferred_element_type=f32)
        for q in range(TILE // LANES):
            total_ref[:, b * (TILE // LANES) + q, :] = totals[:, q * LANES : (q + 1) * LANES]


def column_kernel(parts_ref, sim_ref, out_ref):
    factor = 1.0 / jnp.sum(parts_ref[...], axis=0)
    lhs = two_terms(as_row(factor))
    sums = jnp.dot(lhs, sim_ref[...], preferred_element_type=f32)
    out_ref[...] = jnp.broadcast_to(as_tiles(jnp.sum(sums, axis=0, keepdims=True))[None], out_ref.shape)


def row_kernel(desired_load, parts_ref, sim_ref, out_ref):
    factor = desired_load / jnp.sum(parts_ref[...], axis=0)
    lhs = two_terms(as_row(factor))
    sums = lax.dot_general(lhs, sim_ref[...], (((1,), (1,)), ((), ())), preferred_element_type=f32)
    out_ref[...] = jnp.broadcast_to(as_tiles(jnp.sum(sums, axis=0, keepdims=True))[None], out_ref.shape)


def down(row):
    return jnp.transpose(jnp.broadcast_to(row, (LANES, LANES)))


def numerator_kernel(count, parts_ref, sim_ref, x_ref, out_ref, weight_ref):
    factor = 1.0 / jnp.sum(parts_ref[...], axis=0)
    lhs = two_terms(as_row(factor))
    mass = jnp.sum(jnp.dot(lhs, sim_ref[...], preferred_element_type=f32), axis=0, keepdims=True)
    columns = sim_ref.shape[1]
    for q in range(sim_ref.shape[0] // LANES):
        rows = pl.ds(q * LANES, LANES)
        scale = jnp.concatenate([down(factor[q : q + 1])] * (columns // LANES), axis=1)
        weight_ref[rows, :] = (sim_ref[rows, :].astype(f32) * scale).astype(bf16)
    chunks = x_ref.shape[1] // LANES
    held = columns // out_ref.shape[0]
    base = held * chunks
    for t in range(columns // TILE):
        sums = lax.dot_general(
            weight_ref[:, pl.ds(t * TILE, TILE)],
            x_ref[...],
            (((0,), (0,)), ((), ())),
            preferred_element_type=f32,
        ).astype(bf16)
        for z in range(TILE // count):
            slot, place = divmod(t * TILE + z * count, held)
            for c in range(chunks):
                out_ref[slot, pl.ds(place * chunks + c * count, count), :] = sums[
                    z * count : (z + 1) * count, c * LANES : (c + 1) * LANES
                ]
    for i in range(out_ref.shape[0]):
        own = as_tiles(mass[:, i * held : (i + 1) * held])
        rest = jnp.zeros((out_ref.shape[1] - base - own.shape[0], LANES), f32)
        out_ref[i, pl.ds(base, out_ref.shape[1] - base), :] = jnp.concatenate([own, rest], axis=0).astype(bf16)


def hand_on_kernel(count, parts_ref, out_ref):
    total = jnp.sum(parts_ref[...].astype(f32), axis=0)
    chunk_rows = out_ref.shape[1] - 8
    base = chunk_rows * out_ref.shape[0]
    for z in range(out_ref.shape[0]):
        out_ref[z, pl.ds(0, chunk_rows), :] = total[z * chunk_rows : (z + 1) * chunk_rows].astype(bf16)
        at = z * count % LANES
        row = total[base + z * count // LANES : base + z * count // LANES + 1]
        row = jnp.concatenate([row[:, at:], row[:, :at]], axis=1) if at else row
        out_ref[z, pl.ds(chunk_rows, 8), :] = jnp.broadcast_to(row, (8, LANES)).astype(bf16)


def update_kernel(parts_ref, cent_ref, out_ref):
    total = jnp.sum(parts_ref[...].astype(f32), axis=0)
    count, width = out_ref.shape
    chunk_rows = width // LANES * count
    scale = 1.0 / (down(total[chunk_rows : chunk_rows + 1])[:count] + 1.0)
    for c in range(width // LANES):
        lanes = pl.ds(c * LANES, LANES)
        out_ref[:, lanes] = (total[c * count : (c + 1) * count] + cent_ref[:, lanes]) * scale


def call(kernel, name, operands, outs, mib, flops, scratch=(), hbm_in=(), hbm_out=False):
    moved = sum(math.prod(o.shape) * o.dtype.itemsize for o in (*operands, *outs))
    vmem, hbm = pl.BlockSpec(memory_space=pltpu.VMEM), pl.BlockSpec(memory_space=pltpu.HBM)
    out = hbm if hbm_out else vmem
    single = len(outs) == 1
    if hbm_out:
        outs = [pltpu.HBM(o.shape, o.dtype) for o in outs]
    operands = [
        pltpu.with_memory_space_constraint(o, pltpu.HBM) if i in hbm_in else o
        for i, o in enumerate(operands)
    ]
    return pl.pallas_call(
        kernel,
        name=name,
        out_shape=outs[0] if single else outs,
        in_specs=[hbm if i in hbm_in else vmem for i in range(len(operands))],
        out_specs=out if single else [out] * len(outs),
        scratch_shapes=scratch,
        compiler_params=pltpu.CompilerParams(vmem_limit_bytes=mib * MIB),
        cost_estimate=pl.CostEstimate(flops=flops, bytes_accessed=moved, transcendentals=0),
    )(*operands)


def per_device(embeddings, coarse_ids, centroids, coarse_of):
    row_count, width = embeddings.shape
    local_count = centroids.shape[0]
    near, far, along_z = ("x", "zl"), "zh", ("zh", "zl")
    x_size, near_size, far_size = (lax.axis_size(axes) for axes in ("x", near, far))
    z_size = lax.axis_size(along_z)
    cent_size = lax.axis_size(("y", "core"))
    columns = x_size * z_size * local_count
    desired_load = row_count / (local_count * cent_size)
    layout_table = coarse_of.reshape(x_size, far_size, z_size // far_size, cent_size, local_count)
    group_ids = lax.dynamic_index_in_dim(
        layout_table, lax.axis_index(("y", "core")), 3, keepdims=False
    )
    group_ids = jnp.swapaxes(group_ids, 1, 2).reshape(1, columns)

    array = jax.ShapeDtypeStruct
    unit_like, match_like = array((row_count, width), bf16), array((row_count, columns), bf16)
    blocks = row_count // TILE
    unit_x, matched = call(
        prepare_kernel,
        "prepare",
        (embeddings, coarse_ids.T, group_ids),
        (unit_like, match_like),
        24,
        8 * row_count * CLUSTERS * columns,
        scratch=[
            pltpu.VMEM(unit_like.shape, bf16),
            pltpu.VMEM(unit_like.shape, bf16),
            pltpu.VMEM(match_like.shape, bf16),
            pltpu.VMEM((CLUSTERS, columns), bf16),
            pltpu.SemaphoreType.DMA((3, blocks)),
        ],
        hbm_in=(0,),
        hbm_out=True,
    )
    copies = call(
        unit_copies_kernel, "units", (centroids,), (array((far_size, local_count, width), bf16),), 4, 0
    )
    part = exchange(copies, far)
    copies = call(
        copies_kernel,
        "copies",
        (part, matched),
        (array((near_size,) + part.shape, bf16),),
        4,
        0,
        hbm_in=(1,),
    )
    group_centroids = exchange(copies, near).reshape(columns, width)

    product = 2 * row_count * columns
    row_parts = array((cent_size, row_count // LANES, LANES), f32)
    column_parts = array((x_size, columns // LANES, LANES), f32)
    column_sums = array((z_size, columns // LANES, LANES), f32)
    similarity, parts = call(
        similarity_kernel,
        "similarity",
        (unit_x, group_centroids, matched),
        (match_like, row_parts),
        16,
        product * width,
    )
    parts = exchange(parts, ("y", "core"))
    for sweep in range(SWEEPS):
        parts = call(column_kernel, "columns", (parts, similarity), (column_parts,), 8, product * 16)
        parts = call(sum_copies_kernel, "across", (exchange(parts, "x"),), (column_sums,), 2, 0)
        parts = call(
            functools.partial(row_kernel, desired_load),
            "rows",
            (exchange(parts, along_z), similarity),
            (row_parts,),
            8,
            product * 16,
        )
        parts = exchange(parts, ("y", "core"))
    chunk_rows = width // LANES * local_count
    sums = call(
        functools.partial(numerator_kernel, local_count),
        "numerator",
        (parts, similarity, embeddings),
        (array((near_size, far_size * chunk_rows + 16, LANES), bf16),),
        16,
        product * width,
        scratch=[pltpu.VMEM((row_count, columns), bf16)],
    )
    sums = call(
        functools.partial(hand_on_kernel, local_count),
        "hand_on",
        (exchange(sums, near),),
        (array((far_size, chunk_rows + 8, LANES), bf16),),
        8,
        0,
    )
    return call(
        update_kernel,
        "update",
        (exchange(sums, far), centroids),
        (array(centroids.shape, f32),),
        4,
        0,
    )


def solution(mesh):
    fine = Mesh(mesh.devices.reshape(4, 8, 2, 4, 2), ("x", "zh", "zl", "y", "core"))
    rows, held = P(("x", "zh", "zl"), None), P(("x", "zh", "zl", "y", "core"), None)
    return jax.shard_map(
        per_device,
        mesh=fine,
        in_specs=(rows, rows, held, P()),
        out_specs=held,
        check_vma=False,
    )
```

```python
import functools
import math

import jax
import jax.numpy as jnp
from jax import lax
from jax.experimental import pallas as pl
from jax.experimental.pallas import tpu as pltpu
from jax.sharding import Mesh
from jax.sharding import PartitionSpec as P

SWEEPS = 3
CLUSTERS = 512
LANES = 128
TILE = 256


entropic_smoothing = 0.03
MIB = 1 << 20
f32, bf16 = jnp.float32, jnp.bfloat16


def unit_rows(values):
    values = values.astype(f32)
    return values * lax.rsqrt(jnp.sum(values * values, axis=-1, keepdims=True) + 1e-06)


def exchange(blocks, axes):
    return lax.all_to_all(blocks, axes, 0, 0)


def as_row(tiles):
    return jnp.concatenate([tiles[q : q + 1] for q in range(tiles.shape[0])], axis=1)


def as_tiles(row):
    count = row.shape[1] // LANES
    return jnp.concatenate([row[:, q * LANES : (q + 1) * LANES] for q in range(count)], axis=0)


def two_terms(row):
    wide = jnp.broadcast_to(row, (16, row.shape[1]))
    high = wide.astype(bf16).astype(f32)
    which = lax.broadcasted_iota(jnp.int32, wide.shape, 0)
    rest = jnp.where(which == 1, wide - high, 0.0)
    return jnp.where(which == 0, high, rest).astype(bf16)


def in_turn(blocks, copies, work, ahead=2):
    for b in range(min(ahead, blocks)):
        for copy in copies(b):
            copy.start()
    for b in range(blocks):
        if b + ahead < blocks:
            for copy in copies(b + ahead):
                copy.start()
        for copy in copies(b):
            copy.wait()
        work(b)


def prepare_kernel(x_hbm, ids_ref, group_ref, unit_hbm, match_hbm, x_ref, unit_ref, match_ref, hot_ref, sems):
    blocks = x_ref.shape[0] // TILE
    half = CLUSTERS // 2
    cluster = lax.broadcasted_iota(jnp.int32, hot_ref.shape, 0)
    hot_ref[...] = jnp.where(cluster == group_ref[...], 1.0, 0.0).astype(bf16)
    which = lax.broadcasted_iota(jnp.int32, (half, TILE), 0).astype(f32).astype(bf16)
    which = which.reshape(half // 16, 16, TILE)

    def into(b):
        rows = pl.ds(b * TILE, TILE)
        return (pltpu.make_async_copy(x_hbm.at[rows], x_ref.at[rows], sems.at[0, b]),)

    def out_of(b):
        rows = pl.ds(b * TILE, TILE)
        return (
            pltpu.make_async_copy(unit_ref.at[rows], unit_hbm.at[rows], sems.at[1, b]),
            pltpu.make_async_copy(match_ref.at[rows], match_hbm.at[rows], sems.at[2, b]),
        )

    def work(b):
        rows = pl.ds(b * TILE, TILE)
        unit_ref[rows, :] = unit_rows(x_ref[rows, :]).astype(bf16)
        ids = ids_ref[:, rows]
        matched = jnp.zeros((TILE, match_ref.shape[1]), f32)
        for first in (0, half):
            near = (ids - first).astype(f32)
            picked = jnp.zeros(which.shape, bf16)
            for p in range(ids.shape[0]):
                pick = jnp.broadcast_to(near[p : p + 1], (16, TILE)).astype(bf16)[None]
                picked = jnp.where(pick == which, jnp.ones_like(picked), picked)
            matched += lax.dot_general(
                picked.reshape(half, TILE),
                hot_ref[first : first + half, :],
                (((0,), (0,)), ((), ())),
                preferred_element_type=f32,
            )
        match_ref[rows, :] = matched.astype(bf16)
        for copy in out_of(b):
            copy.start()

    in_turn(blocks, into, work)
    for b in range(blocks):
        for copy in out_of(b):
            copy.wait()


def unit_copies_kernel(cent_hbm, out_hbm, cent_ref, unit_ref, sems):
    count = out_hbm.shape[0]
    fetch = pltpu.make_async_copy(cent_hbm, cent_ref, sems.at[count])
    fetch.start()
    fetch.wait()
    unit_ref[...] = unit_rows(cent_ref[...]).astype(bf16)
    copies = [pltpu.make_async_copy(unit_ref, out_hbm.at[i], sems.at[i]) for i in range(count)]
    for copy in copies:
        copy.start()
    for copy in copies:
        copy.wait()


def copies_kernel(block_ref, unused, out_ref):
    for i in range(out_ref.shape[0]):
        out_ref[i] = block_ref[...]


def sum_copies_kernel(parts_ref, out_ref):
    out_ref[...] = jnp.broadcast_to(jnp.sum(parts_ref[...], axis=0)[None], out_ref.shape)


def similarity_kernel(unit_ref, cent_ref, match_ref, sim_ref, total_ref):
    ones = jnp.ones((total_ref.shape[0], sim_ref.shape[1]), bf16)
    scale = math.log2(math.e) / entropic_smoothing
    for b in range(unit_ref.shape[0] // TILE):
        rows = pl.ds(b * TILE, TILE)
        dots = lax.dot_general(
            unit_ref[rows, :], cent_ref[...], (((1,), (1,)), ((), ())), preferred_element_type=f32
        )
        sim = (jnp.exp2(dots * scale) * match_ref[rows, :].astype(f32)).astype(bf16)
        sim_ref[rows, :] = sim
        totals = lax.dot_general(ones, sim, (((1,), (1,)), ((), ())), preferred_element_type=f32)
        for q in range(TILE // LANES):
            total_ref[:, b * (TILE // LANES) + q, :] = totals[:, q * LANES : (q + 1) * LANES]


def column_kernel(parts_ref, sim_ref, out_ref):
    factor = 1.0 / jnp.sum(parts_ref[...], axis=0)
    lhs = two_terms(as_row(factor))
    sums = jnp.dot(lhs, sim_ref[...], preferred_element_type=f32)
    out_ref[...] = jnp.broadcast_to(as_tiles(jnp.sum(sums, axis=0, keepdims=True))[None], out_ref.shape)


def row_kernel(desired_load, parts_ref, sim_ref, out_ref):
    factor = desired_load / jnp.sum(parts_ref[...], axis=0)
    lhs = two_terms(as_row(factor))
    sums = lax.dot_general(lhs, sim_ref[...], (((1,), (1,)), ((), ())), preferred_element_type=f32)
    out_ref[...] = jnp.broadcast_to(as_tiles(jnp.sum(sums, axis=0, keepdims=True))[None], out_ref.shape)


def down(row):
    return jnp.transpose(jnp.broadcast_to(row, (LANES, LANES)))


def numerator_kernel(count, parts_ref, sim_ref, x_ref, out_ref, weight_ref):
    factor = 1.0 / jnp.sum(parts_ref[...], axis=0)
    columns = sim_ref.shape[1]
    mass = jnp.zeros((8, columns), f32)
    for q in range(sim_ref.shape[0] // LANES):
        rows = pl.ds(q * LANES, LANES)
        scale = jnp.concatenate([down(factor[q : q + 1])] * (columns // LANES), axis=1)
        weight = sim_ref[rows, :].astype(f32) * scale
        weight_ref[rows, :] = weight.astype(bf16)
        mass += jnp.sum(weight.reshape(LANES // 8, 8, columns), axis=0)
    mass = jnp.sum(mass, axis=0, keepdims=True)
    chunks = x_ref.shape[1] // LANES
    held = columns // out_ref.shape[0]
    base = held * chunks
    for t in range(columns // TILE):
        sums = lax.dot_general(
            weight_ref[:, pl.ds(t * TILE, TILE)],
            x_ref[...],
            (((0,), (0,)), ((), ())),
            preferred_element_type=f32,
        ).astype(bf16)
        for z in range(TILE // count):
            slot, place = divmod(t * TILE + z * count, held)
            for c in range(chunks):
                out_ref[slot, pl.ds(place * chunks + c * count, count), :] = sums[
                    z * count : (z + 1) * count, c * LANES : (c + 1) * LANES
                ]
    for i in range(out_ref.shape[0]):
        own = as_tiles(mass[:, i * held : (i + 1) * held])
        rest = jnp.zeros((out_ref.shape[1] - base - own.shape[0], LANES), f32)
        out_ref[i, pl.ds(base, out_ref.shape[1] - base), :] = jnp.concatenate([own, rest], axis=0).astype(bf16)


def hand_on_kernel(count, parts_ref, out_ref):
    total = jnp.sum(parts_ref[...].astype(f32), axis=0)
    chunk_rows = out_ref.shape[1] - 8
    base = chunk_rows * out_ref.shape[0]
    for z in range(out_ref.shape[0]):
        out_ref[z, pl.ds(0, chunk_rows), :] = total[z * chunk_rows : (z + 1) * chunk_rows].astype(bf16)
        at = z * count % LANES
        row = total[base + z * count // LANES : base + z * count // LANES + 1]
        row = jnp.concatenate([row[:, at:], row[:, :at]], axis=1) if at else row
        out_ref[z, pl.ds(chunk_rows, 8), :] = jnp.broadcast_to(row, (8, LANES)).astype(bf16)


def update_kernel(parts_ref, cent_ref, out_ref):
    total = jnp.sum(parts_ref[...].astype(f32), axis=0)
    count, width = out_ref.shape
    chunk_rows = width // LANES * count
    scale = 1.0 / (down(total[chunk_rows : chunk_rows + 1])[:count] + 1.0)
    for c in range(width // LANES):
        lanes = pl.ds(c * LANES, LANES)
        out_ref[:, lanes] = (total[c * count : (c + 1) * count] + cent_ref[:, lanes]) * scale


def call(kernel, name, operands, outs, mib, flops, scratch=(), hbm_in=(), hbm_out=False):
    moved = sum(math.prod(o.shape) * o.dtype.itemsize for o in (*operands, *outs))
    vmem, hbm = pl.BlockSpec(memory_space=pltpu.VMEM), pl.BlockSpec(memory_space=pltpu.HBM)
    out = hbm if hbm_out else vmem
    single = len(outs) == 1
    if hbm_out:
        outs = tuple(pltpu.HBM(o.shape, o.dtype) for o in outs)
    operands = [
        pltpu.with_memory_space_constraint(o, pltpu.HBM) if i in hbm_in else o
        for i, o in enumerate(operands)
    ]
    return pl.pallas_call(
        kernel,
        name=name,
        out_shape=outs[0] if single else outs,
        in_specs=[hbm if i in hbm_in else vmem for i in range(len(operands))],
        out_specs=out if single else [out] * len(outs),
        scratch_shapes=scratch,
        compiler_params=pltpu.CompilerParams(vmem_limit_bytes=mib * MIB),
        cost_estimate=pl.CostEstimate(flops=flops, bytes_accessed=moved, transcendentals=0),
    )(*operands)


def per_device(embeddings, coarse_ids, centroids, coarse_of):
    row_count, width = embeddings.shape
    local_count = centroids.shape[0]
    near, far, along_z = ("x", "zl"), "zh", ("zh", "zl")
    x_size, near_size, far_size = (lax.axis_size(axes) for axes in ("x", near, far))
    z_size = lax.axis_size(along_z)
    cent_size = lax.axis_size(("y", "core"))
    columns = x_size * z_size * local_count
    desired_load = row_count / (local_count * cent_size)
    layout_table = coarse_of.reshape(x_size, far_size, z_size // far_size, cent_size, local_count)
    group_ids = lax.dynamic_index_in_dim(
        layout_table, lax.axis_index(("y", "core")), 3, keepdims=False
    )
    group_ids = jnp.swapaxes(group_ids, 1, 2).reshape(1, columns)

    array = jax.ShapeDtypeStruct
    unit_like, match_like = array((row_count, width), bf16), array((row_count, columns), bf16)
    blocks = row_count // TILE
    unit_x, matched = call(
        prepare_kernel,
        "prepare",
        (embeddings, coarse_ids.T, group_ids),
        (unit_like, match_like),
        24,
        8 * row_count * CLUSTERS * columns,
        scratch=[
            pltpu.VMEM(unit_like.shape, bf16),
            pltpu.VMEM(unit_like.shape, bf16),
            pltpu.VMEM(match_like.shape, bf16),
            pltpu.VMEM((CLUSTERS, columns), bf16),
            pltpu.SemaphoreType.DMA((3, blocks)),
        ],
        hbm_in=(0,),
        hbm_out=True,
    )
    copies = call(
        unit_copies_kernel,
        "units",
        (centroids,),
        (array((far_size, local_count, width), bf16),),
        4,
        0,
        scratch=[
            pltpu.VMEM(centroids.shape, f32),
            pltpu.VMEM(centroids.shape, bf16),
            pltpu.SemaphoreType.DMA((far_size + 1,)),
        ],
        hbm_in=(0,),
        hbm_out=True,
    )
    part = exchange(copies, far)
    copies = call(
        copies_kernel,
        "copies",
        (part, matched),
        (array((near_size,) + part.shape, bf16),),
        4,
        0,
        hbm_in=(1,),
    )
    group_centroids = exchange(copies, near).reshape(columns, width)

    product = 2 * row_count * columns
    row_parts = array((cent_size, row_count // LANES, LANES), f32)
    column_parts = array((x_size, columns // LANES, LANES), f32)
    column_sums = array((z_size, columns // LANES, LANES), f32)
    similarity, parts = call(
        similarity_kernel,
        "similarity",
        (unit_x, group_centroids, matched),
        (match_like, row_parts),
        16,
        product * width,
    )
    parts = exchange(parts, ("y", "core"))
    for sweep in range(SWEEPS):
        parts = call(column_kernel, "columns", (parts, similarity), (column_parts,), 8, product * 16)
        parts = call(sum_copies_kernel, "across", (exchange(parts, "x"),), (column_sums,), 2, 0)
        parts = call(
            functools.partial(row_kernel, desired_load),
            "rows",
            (exchange(parts, along_z), similarity),
            (row_parts,),
            8,
            product * 16,
        )
        parts = exchange(parts, ("y", "core"))
    chunk_rows = width // LANES * local_count
    sums = call(
        functools.partial(numerator_kernel, local_count),
        "numerator",
        (parts, similarity, embeddings),
        (array((near_size, far_size * chunk_rows + 16, LANES), bf16),),
        16,
        product * width,
        scratch=[pltpu.VMEM((row_count, columns), bf16)],
    )
    sums = call(
        functools.partial(hand_on_kernel, local_count),
        "hand_on",
        (exchange(sums, near),),
        (array((far_size, chunk_rows + 8, LANES), bf16),),
        8,
        0,
    )
    return call(
        update_kernel,
        "update",
        (exchange(sums, far), centroids),
        (array(centroids.shape, f32),),
        4,
        0,
    )


def solution(mesh):
    fine = Mesh(mesh.devices.reshape(4, 8, 2, 4, 2), ("x", "zh", "zl", "y", "core"))
    rows, held = P(("x", "zh", "zl"), None), P(("x", "zh", "zl", "y", "core"), None)
    return jax.shard_map(
        per_device,
        mesh=fine,
        in_specs=(rows, rows, held, P()),
        out_specs=held,
        check_vma=False,
    )
```

```python
import functools
import math

import jax
import jax.numpy as jnp
from jax import lax
from jax.experimental import pallas as pl
from jax.experimental.pallas import tpu as pltpu
from jax.sharding import Mesh
from jax.sharding import PartitionSpec as P

SWEEPS = 3
CLUSTERS = 512
LANES = 128
TILE = 256


entropic_smoothing = 0.03
MIB = 1 << 20
f32, bf16 = jnp.float32, jnp.bfloat16


def unit_rows(values):
    values = values.astype(f32)
    return values * lax.rsqrt(jnp.sum(values * values, axis=-1, keepdims=True) + 1e-06)


def exchange(blocks, axes):
    return lax.all_to_all(blocks, axes, 0, 0)


def as_row(tiles):
    return jnp.concatenate([tiles[q : q + 1] for q in range(tiles.shape[0])], axis=1)


def as_tiles(row):
    count = row.shape[1] // LANES
    return jnp.concatenate([row[:, q * LANES : (q + 1) * LANES] for q in range(count)], axis=0)


def two_terms(row):
    wide = jnp.broadcast_to(row, (16, row.shape[1]))
    high = wide.astype(bf16).astype(f32)
    which = lax.broadcasted_iota(jnp.int32, wide.shape, 0)
    rest = jnp.where(which == 1, wide - high, 0.0)
    return jnp.where(which == 0, high, rest).astype(bf16)


def in_turn(blocks, copies, work, ahead=2):
    for b in range(min(ahead, blocks)):
        for copy in copies(b):
            copy.start()
    for b in range(blocks):
        if b + ahead < blocks:
            for copy in copies(b + ahead):
                copy.start()
        for copy in copies(b):
            copy.wait()
        work(b)


def prepare_kernel(x_hbm, ids_ref, group_ref, unit_hbm, match_hbm, x_ref, unit_ref, match_ref, hot_ref, sems):
    blocks = x_ref.shape[0] // TILE
    half = CLUSTERS // 2
    cluster = lax.broadcasted_iota(jnp.int32, hot_ref.shape, 0)
    hot_ref[...] = jnp.where(cluster == group_ref[...], 1.0, 0.0).astype(bf16)
    which = lax.broadcasted_iota(jnp.int32, (half, TILE), 0).astype(f32).astype(bf16)
    which = which.reshape(half // 16, 16, TILE)

    def into(b):
        rows = pl.ds(b * TILE, TILE)
        return (pltpu.make_async_copy(x_hbm.at[rows], x_ref.at[rows], sems.at[0, b]),)

    def out_of(b):
        rows = pl.ds(b * TILE, TILE)
        return (
            pltpu.make_async_copy(unit_ref.at[rows], unit_hbm.at[rows], sems.at[1, b]),
            pltpu.make_async_copy(match_ref.at[rows], match_hbm.at[rows], sems.at[2, b]),
        )

    def work(b):
        rows = pl.ds(b * TILE, TILE)
        unit_ref[rows, :] = unit_rows(x_ref[rows, :]).astype(bf16)
        ids = ids_ref[:, rows]
        matched = jnp.zeros((TILE, match_ref.shape[1]), f32)
        for first in (0, half):
            near = (ids - first).astype(f32)
            picked = jnp.zeros(which.shape, bf16)
            for p in range(ids.shape[0]):
                pick = jnp.broadcast_to(near[p : p + 1], (16, TILE)).astype(bf16)[None]
                picked = jnp.where(pick == which, jnp.ones_like(picked), picked)
            matched += lax.dot_general(
                picked.reshape(half, TILE),
                hot_ref[first : first + half, :],
                (((0,), (0,)), ((), ())),
                preferred_element_type=f32,
            )
        match_ref[rows, :] = matched.astype(bf16)
        for copy in out_of(b):
            copy.start()

    in_turn(blocks, into, work)
    for b in range(blocks):
        for copy in out_of(b):
            copy.wait()


def unit_copies_kernel(cent_ref, out_ref):
    out_ref[...] = jnp.broadcast_to(unit_rows(cent_ref[...]).astype(bf16)[None], out_ref.shape)


def copies_kernel(block_ref, unused, out_ref):
    for i in range(out_ref.shape[0]):
        out_ref[i] = block_ref[...]


def sum_copies_kernel(parts_ref, out_ref):
    out_ref[...] = jnp.broadcast_to(jnp.sum(parts_ref[...], axis=0)[None], out_ref.shape)


def similarity_kernel(unit_ref, cent_ref, match_ref, sim_ref, total_ref):
    ones = jnp.ones((total_ref.shape[0], sim_ref.shape[1]), bf16)
    scale = math.log2(math.e) / entropic_smoothing
    for b in range(unit_ref.shape[0] // TILE):
        rows = pl.ds(b * TILE, TILE)
        dots = lax.dot_general(
            unit_ref[rows, :], cent_ref[...], (((1,), (1,)), ((), ())), preferred_element_type=f32
        )
        sim = (jnp.exp2(dots * scale) * match_ref[rows, :].astype(f32)).astype(bf16)
        sim_ref[rows, :] = sim
        totals = lax.dot_general(ones, sim, (((1,), (1,)), ((), ())), preferred_element_type=f32)
        for q in range(TILE // LANES):
            total_ref[:, b * (TILE // LANES) + q, :] = totals[:, q * LANES : (q + 1) * LANES]


def column_kernel(parts_ref, sim_ref, out_ref):
    factor = 1.0 / jnp.sum(parts_ref[...], axis=0)
    lhs = two_terms(as_row(factor))
    sums = jnp.dot(lhs, sim_ref[...], preferred_element_type=f32)
    out_ref[...] = jnp.broadcast_to(as_tiles(jnp.sum(sums, axis=0, keepdims=True))[None], out_ref.shape)


def row_kernel(desired_load, parts_ref, sim_ref, out_ref):
    factor = desired_load / jnp.sum(parts_ref[...], axis=0)
    lhs = two_terms(as_row(factor))
    sums = lax.dot_general(lhs, sim_ref[...], (((1,), (1,)), ((), ())), preferred_element_type=f32)
    out_ref[...] = jnp.broadcast_to(as_tiles(jnp.sum(sums, axis=0, keepdims=True))[None], out_ref.shape)


def down(row):
    return jnp.transpose(jnp.broadcast_to(row, (LANES, LANES)))


def numerator_kernel(count, parts_ref, sim_ref, x_ref, out_ref, weight_ref):
    factor = 1.0 / jnp.sum(parts_ref[...], axis=0)
    lhs = two_terms(as_row(factor))
    mass = jnp.sum(jnp.dot(lhs, sim_ref[...], preferred_element_type=f32), axis=0, keepdims=True)
    columns = sim_ref.shape[1]
    for q in range(sim_ref.shape[0] // LANES):
        rows = pl.ds(q * LANES, LANES)
        scale = jnp.concatenate([down(factor[q : q + 1])] * (columns // LANES), axis=1)
        weight_ref[rows, :] = (sim_ref[rows, :].astype(f32) * scale).astype(bf16)
    chunks = x_ref.shape[1] // LANES
    held = columns // out_ref.shape[0]
    base = held * chunks
    for t in range(columns // TILE):
        sums = lax.dot_general(
            weight_ref[:, pl.ds(t * TILE, TILE)],
            x_ref[...],
            (((0,), (0,)), ((), ())),
            preferred_element_type=f32,
        ).astype(bf16)
        for z in range(TILE // count):
            slot, place = divmod(t * TILE + z * count, held)
            for c in range(chunks):
                out_ref[slot, pl.ds(place * chunks + c * count, count), :] = sums[
                    z * count : (z + 1) * count, c * LANES : (c + 1) * LANES
                ]
    for i in range(out_ref.shape[0]):
        own = as_tiles(mass[:, i * held : (i + 1) * held])
        rest = jnp.zeros((out_ref.shape[1] - base - own.shape[0], LANES), f32)
        out_ref[i, pl.ds(base, out_ref.shape[1] - base), :] = jnp.concatenate([own, rest], axis=0).astype(bf16)


def hand_on_kernel(count, parts_ref, out_ref):
    total = jnp.sum(parts_ref[...].astype(f32), axis=0)
    chunk_rows = out_ref.shape[1] - 8
    base = chunk_rows * out_ref.shape[0]
    for z in range(out_ref.shape[0]):
        out_ref[z, pl.ds(0, chunk_rows), :] = total[z * chunk_rows : (z + 1) * chunk_rows].astype(bf16)
        at = z * count % LANES
        row = total[base + z * count // LANES : base + z * count // LANES + 1]
        row = jnp.concatenate([row[:, at:], row[:, :at]], axis=1) if at else row
        out_ref[z, pl.ds(chunk_rows, 8), :] = jnp.broadcast_to(row, (8, LANES)).astype(bf16)


def update_kernel(parts_ref, cent_ref, out_ref):
    total = jnp.sum(parts_ref[...].astype(f32), axis=0)
    count, width = out_ref.shape
    chunk_rows = width // LANES * count
    scale = 1.0 / (down(total[chunk_rows : chunk_rows + 1])[:count] + 1.0)
    for c in range(width // LANES):
        lanes = pl.ds(c * LANES, LANES)
        out_ref[:, lanes] = (total[c * count : (c + 1) * count] + cent_ref[:, lanes]) * scale


def call(kernel, name, operands, outs, mib, flops, scratch=(), hbm_in=(), hbm_out=False):
    moved = sum(math.prod(o.shape) * o.dtype.itemsize for o in (*operands, *outs))
    vmem, hbm = pl.BlockSpec(memory_space=pltpu.VMEM), pl.BlockSpec(memory_space=pltpu.HBM)
    out = hbm if hbm_out else vmem
    single = len(outs) == 1
    if hbm_out:
        outs = [pltpu.HBM(o.shape, o.dtype) for o in outs]
    operands = [
        pltpu.with_memory_space_constraint(o, pltpu.HBM) if i in hbm_in else o
        for i, o in enumerate(operands)
    ]
    return pl.pallas_call(
        kernel,
        name=name,
        out_shape=outs[0] if single else outs,
        in_specs=[hbm if i in hbm_in else vmem for i in range(len(operands))],
        out_specs=out if single else [out] * len(outs),
        scratch_shapes=scratch,
        compiler_params=pltpu.CompilerParams(vmem_limit_bytes=mib * MIB),
        cost_estimate=pl.CostEstimate(flops=flops, bytes_accessed=moved, transcendentals=0),
    )(*operands)


def per_device(embeddings, coarse_ids, centroids, coarse_of):
    row_count, width = embeddings.shape
    local_count = centroids.shape[0]
    near, far, along_z = ("x", "zl"), "zh", ("zh", "zl")
    x_size, near_size, far_size = (lax.axis_size(axes) for axes in ("x", near, far))
    z_size = lax.axis_size(along_z)
    cent_size = lax.axis_size(("y", "core"))
    columns = x_size * z_size * local_count
    desired_load = row_count / (local_count * cent_size)
    layout_table = coarse_of.reshape(x_size, far_size, z_size // far_size, cent_size, local_count)
    group_ids = lax.dynamic_index_in_dim(
        layout_table, lax.axis_index(("y", "core")), 3, keepdims=False
    )
    group_ids = jnp.swapaxes(group_ids, 1, 2).reshape(1, columns)

    array = jax.ShapeDtypeStruct
    unit_like, match_like = array((row_count, width), bf16), array((row_count, columns), bf16)
    blocks = row_count // TILE
    unit_x, matched = call(
        prepare_kernel,
        "prepare",
        (embeddings, coarse_ids.T, group_ids),
        (unit_like, match_like),
        24,
        8 * row_count * CLUSTERS * columns,
        scratch=[
            pltpu.VMEM(unit_like.shape, bf16),
            pltpu.VMEM(unit_like.shape, bf16),
            pltpu.VMEM(match_like.shape, bf16),
            pltpu.VMEM((CLUSTERS, columns), bf16),
            pltpu.SemaphoreType.DMA((3, blocks)),
        ],
        hbm_in=(0,),
        hbm_out=True,
    )
    copies = call(
        unit_copies_kernel, "units", (centroids,), (array((far_size, local_count, width), bf16),), 4, 0
    )
    part = exchange(copies, far)
    copies = call(
        copies_kernel,
        "copies",
        (part, matched),
        (array((near_size,) + part.shape, bf16),),
        4,
        0,
        hbm_in=(1,),
    )
    group_centroids = exchange(copies, near).reshape(columns, width)

    product = 2 * row_count * columns
    row_parts = array((cent_size, row_count // LANES, LANES), f32)
    column_parts = array((near_size, columns // LANES, LANES), f32)
    column_sums = array((far_size, columns // LANES, LANES), f32)
    similarity, parts = call(
        similarity_kernel,
        "similarity",
        (unit_x, group_centroids, matched),
        (match_like, row_parts),
        16,
        product * width,
    )
    parts = exchange(parts, ("y", "core"))
    for sweep in range(SWEEPS):
        parts = call(column_kernel, "columns", (parts, similarity), (column_parts,), 8, product * 16)
        parts = call(sum_copies_kernel, "across", (exchange(parts, near),), (column_sums,), 2, 0)
        parts = call(
            functools.partial(row_kernel, desired_load),
            "rows",
            (exchange(parts, far), similarity),
            (row_parts,),
            8,
            product * 16,
        )
        parts = exchange(parts, ("y", "core"))
    chunk_rows = width // LANES * local_count
    sums = call(
        functools.partial(numerator_kernel, local_count),
        "numerator",
        (parts, similarity, embeddings),
        (array((near_size, far_size * chunk_rows + 16, LANES), bf16),),
        16,
        product * width,
        scratch=[pltpu.VMEM((row_count, columns), bf16)],
    )
    sums = call(
        functools.partial(hand_on_kernel, local_count),
        "hand_on",
        (exchange(sums, near),),
        (array((far_size, chunk_rows + 8, LANES), bf16),),
        8,
        0,
    )
    return call(
        update_kernel,
        "update",
        (exchange(sums, far), centroids),
        (array(centroids.shape, f32),),
        4,
        0,
    )


def solution(mesh):
    fine = Mesh(mesh.devices.reshape(4, 8, 2, 4, 2), ("x", "zh", "zl", "y", "core"))
    rows, held = P(("x", "zh", "zl"), None), P(("x", "zh", "zl", "y", "core"), None)
    return jax.shard_map(
        per_device,
        mesh=fine,
        in_specs=(rows, rows, held, P()),
        out_specs=held,
        check_vma=False,
    )
```

```python
import functools
import math

import jax
import jax.numpy as jnp
from jax import lax
from jax.experimental import pallas as pl
from jax.experimental.pallas import tpu as pltpu
from jax.sharding import Mesh
from jax.sharding import PartitionSpec as P

SWEEPS = 3
CLUSTERS = 512
LANES = 128
TILE = 256


entropic_smoothing = 0.03
MIB = 1 << 20
f32, bf16 = jnp.float32, jnp.bfloat16


def unit_rows(values):
    values = values.astype(f32)
    return values * lax.rsqrt(jnp.sum(values * values, axis=-1, keepdims=True) + 1e-06)


def exchange(blocks, axes):
    return lax.all_to_all(blocks, axes, 0, 0)


def as_row(tiles):
    return jnp.concatenate([tiles[q : q + 1] for q in range(tiles.shape[0])], axis=1)


def as_tiles(row):
    count = row.shape[1] // LANES
    return jnp.concatenate([row[:, q * LANES : (q + 1) * LANES] for q in range(count)], axis=0)


def two_terms(row):
    wide = jnp.broadcast_to(row, (16, row.shape[1]))
    high = wide.astype(bf16).astype(f32)
    which = lax.broadcasted_iota(jnp.int32, wide.shape, 0)
    rest = jnp.where(which == 1, wide - high, 0.0)
    return jnp.where(which == 0, high, rest).astype(bf16)


def in_turn(blocks, copies, work, ahead=2):
    for b in range(min(ahead, blocks)):
        for copy in copies(b):
            copy.start()
    for b in range(blocks):
        if b + ahead < blocks:
            for copy in copies(b + ahead):
                copy.start()
        for copy in copies(b):
            copy.wait()
        work(b)


def prepare_kernel(x_hbm, ids_ref, group_ref, unit_hbm, match_hbm, x_ref, unit_ref, match_ref, hot_ref, sems):
    blocks = x_ref.shape[0] // TILE
    half = CLUSTERS // 2
    cluster = lax.broadcasted_iota(jnp.int32, hot_ref.shape, 0)
    hot_ref[...] = jnp.where(cluster == group_ref[...], 1.0, 0.0).astype(bf16)
    which = lax.broadcasted_iota(jnp.int32, (half, TILE), 0).astype(f32).astype(bf16)
    which = which.reshape(half // 16, 16, TILE)

    def into(b):
        rows = pl.ds(b * TILE, TILE)
        return (pltpu.make_async_copy(x_hbm.at[rows], x_ref.at[rows], sems.at[0, b]),)

    def out_of(b):
        rows = pl.ds(b * TILE, TILE)
        return (
            pltpu.make_async_copy(unit_ref.at[rows], unit_hbm.at[rows], sems.at[1, b]),
            pltpu.make_async_copy(match_ref.at[rows], match_hbm.at[rows], sems.at[2, b]),
        )

    def work(b):
        rows = pl.ds(b * TILE, TILE)
        unit_ref[rows, :] = unit_rows(x_ref[rows, :]).astype(bf16)
        ids = ids_ref[:, rows]
        matched = jnp.zeros((TILE, match_ref.shape[1]), f32)
        for first in (0, half):
            near = (ids - first).astype(f32)
            picked = jnp.zeros(which.shape, bf16)
            for p in range(ids.shape[0]):
                pick = jnp.broadcast_to(near[p : p + 1], (16, TILE)).astype(bf16)[None]
                picked = jnp.where(pick == which, jnp.ones_like(picked), picked)
            matched += lax.dot_general(
                picked.reshape(half, TILE),
                hot_ref[first : first + half, :],
                (((0,), (0,)), ((), ())),
                preferred_element_type=f32,
            )
        match_ref[rows, :] = matched.astype(bf16)
        for copy in out_of(b):
            copy.start()

    in_turn(blocks, into, work)
    for b in range(blocks):
        for copy in out_of(b):
            copy.wait()


def unit_copies_kernel(cent_ref, out_ref):
    out_ref[...] = jnp.broadcast_to(unit_rows(cent_ref[...]).astype(bf16)[None], out_ref.shape)


def copies_kernel(block_ref, unused, out_ref):
    for i in range(out_ref.shape[0]):
        out_ref[i] = block_ref[...]


def sum_copies_kernel(parts_ref, out_ref):
    out_ref[...] = jnp.broadcast_to(jnp.sum(parts_ref[...], axis=0)[None], out_ref.shape)


def similarity_kernel(unit_ref, cent_ref, match_ref, sim_ref, total_ref):
    ones = jnp.ones((total_ref.shape[0], sim_ref.shape[1]), bf16)
    scale = math.log2(math.e) / entropic_smoothing
    step = 2 * TILE
    for b in range(unit_ref.shape[0] // step):
        rows = pl.ds(b * step, step)
        dots = lax.dot_general(
            unit_ref[rows, :], cent_ref[...], (((1,), (1,)), ((), ())), preferred_element_type=f32
        )
        sim = (jnp.exp2(dots * scale) * match_ref[rows, :].astype(f32)).astype(bf16)
        sim_ref[rows, :] = sim
        totals = lax.dot_general(ones, sim, (((1,), (1,)), ((), ())), preferred_element_type=f32)
        for q in range(step // LANES):
            total_ref[:, b * (step // LANES) + q, :] = totals[:, q * LANES : (q + 1) * LANES]


def column_kernel(parts_ref, sim_ref, out_ref):
    factor = 1.0 / jnp.sum(parts_ref[...], axis=0)
    lhs = two_terms(as_row(factor))
    sums = jnp.dot(lhs, sim_ref[...], preferred_element_type=f32)
    out_ref[...] = jnp.broadcast_to(as_tiles(jnp.sum(sums, axis=0, keepdims=True))[None], out_ref.shape)


def row_kernel(desired_load, parts_ref, sim_ref, out_ref):
    factor = desired_load / jnp.sum(parts_ref[...], axis=0)
    lhs = two_terms(as_row(factor))
    sums = lax.dot_general(lhs, sim_ref[...], (((1,), (1,)), ((), ())), preferred_element_type=f32)
    out_ref[...] = jnp.broadcast_to(as_tiles(jnp.sum(sums, axis=0, keepdims=True))[None], out_ref.shape)


def down(row):
    return jnp.transpose(jnp.broadcast_to(row, (LANES, LANES)))


def numerator_kernel(count, parts_ref, sim_ref, x_ref, out_ref, weight_ref):
    factor = 1.0 / jnp.sum(parts_ref[...], axis=0)
    lhs = two_terms(as_row(factor))
    mass = jnp.sum(jnp.dot(lhs, sim_ref[...], preferred_element_type=f32), axis=0, keepdims=True)
    columns = sim_ref.shape[1]
    for q in range(sim_ref.shape[0] // LANES):
        rows = pl.ds(q * LANES, LANES)
        scale = jnp.concatenate([down(factor[q : q + 1])] * (columns // LANES), axis=1)
        weight_ref[rows, :] = (sim_ref[rows, :].astype(f32) * scale).astype(bf16)
    chunks = x_ref.shape[1] // LANES
    held = columns // out_ref.shape[0]
    base = held * chunks
    for t in range(columns // TILE):
        sums = lax.dot_general(
            weight_ref[:, pl.ds(t * TILE, TILE)],
            x_ref[...],
            (((0,), (0,)), ((), ())),
            preferred_element_type=f32,
        ).astype(bf16)
        for z in range(TILE // count):
            slot, place = divmod(t * TILE + z * count, held)
            for c in range(chunks):
                out_ref[slot, pl.ds(place * chunks + c * count, count), :] = sums[
                    z * count : (z + 1) * count, c * LANES : (c + 1) * LANES
                ]
    for i in range(out_ref.shape[0]):
        own = as_tiles(mass[:, i * held : (i + 1) * held])
        rest = jnp.zeros((out_ref.shape[1] - base - own.shape[0], LANES), f32)
        out_ref[i, pl.ds(base, out_ref.shape[1] - base), :] = jnp.concatenate([own, rest], axis=0).astype(bf16)


def hand_on_kernel(count, parts_ref, out_ref):
    total = jnp.sum(parts_ref[...].astype(f32), axis=0)
    chunk_rows = out_ref.shape[1] - 8
    base = chunk_rows * out_ref.shape[0]
    for z in range(out_ref.shape[0]):
        out_ref[z, pl.ds(0, chunk_rows), :] = total[z * chunk_rows : (z + 1) * chunk_rows].astype(bf16)
        at = z * count % LANES
        row = total[base + z * count // LANES : base + z * count // LANES + 1]
        row = jnp.concatenate([row[:, at:], row[:, :at]], axis=1) if at else row
        out_ref[z, pl.ds(chunk_rows, 8), :] = jnp.broadcast_to(row, (8, LANES)).astype(bf16)


def update_kernel(parts_ref, cent_ref, out_ref):
    total = jnp.sum(parts_ref[...].astype(f32), axis=0)
    count, width = out_ref.shape
    chunk_rows = width // LANES * count
    scale = 1.0 / (down(total[chunk_rows : chunk_rows + 1])[:count] + 1.0)
    for c in range(width // LANES):
        lanes = pl.ds(c * LANES, LANES)
        out_ref[:, lanes] = (total[c * count : (c + 1) * count] + cent_ref[:, lanes]) * scale


def call(kernel, name, operands, outs, mib, flops, scratch=(), hbm_in=(), hbm_out=False):
    moved = sum(math.prod(o.shape) * o.dtype.itemsize for o in (*operands, *outs))
    vmem, hbm = pl.BlockSpec(memory_space=pltpu.VMEM), pl.BlockSpec(memory_space=pltpu.HBM)
    out = hbm if hbm_out else vmem
    single = len(outs) == 1
    if hbm_out:
        outs = [pltpu.HBM(o.shape, o.dtype) for o in outs]
    operands = [
        pltpu.with_memory_space_constraint(o, pltpu.HBM) if i in hbm_in else o
        for i, o in enumerate(operands)
    ]
    return pl.pallas_call(
        kernel,
        name=name,
        out_shape=outs[0] if single else outs,
        in_specs=[hbm if i in hbm_in else vmem for i in range(len(operands))],
        out_specs=out if single else [out] * len(outs),
        scratch_shapes=scratch,
        compiler_params=pltpu.CompilerParams(vmem_limit_bytes=mib * MIB),
        cost_estimate=pl.CostEstimate(flops=flops, bytes_accessed=moved, transcendentals=0),
    )(*operands)


def per_device(embeddings, coarse_ids, centroids, coarse_of):
    row_count, width = embeddings.shape
    local_count = centroids.shape[0]
    near, far, along_z = ("x", "zl"), "zh", ("zh", "zl")
    x_size, near_size, far_size = (lax.axis_size(axes) for axes in ("x", near, far))
    z_size = lax.axis_size(along_z)
    cent_size = lax.axis_size(("y", "core"))
    columns = x_size * z_size * local_count
    desired_load = row_count / (local_count * cent_size)
    layout_table = coarse_of.reshape(x_size, far_size, z_size // far_size, cent_size, local_count)
    group_ids = lax.dynamic_index_in_dim(
        layout_table, lax.axis_index(("y", "core")), 3, keepdims=False
    )
    group_ids = jnp.swapaxes(group_ids, 1, 2).reshape(1, columns)

    array = jax.ShapeDtypeStruct
    unit_like, match_like = array((row_count, width), bf16), array((row_count, columns), bf16)
    blocks = row_count // TILE
    unit_x, matched = call(
        prepare_kernel,
        "prepare",
        (embeddings, coarse_ids.T, group_ids),
        (unit_like, match_like),
        24,
        8 * row_count * CLUSTERS * columns,
        scratch=[
            pltpu.VMEM(unit_like.shape, bf16),
            pltpu.VMEM(unit_like.shape, bf16),
            pltpu.VMEM(match_like.shape, bf16),
            pltpu.VMEM((CLUSTERS, columns), bf16),
            pltpu.SemaphoreType.DMA((3, blocks)),
        ],
        hbm_in=(0,),
        hbm_out=True,
    )
    copies = call(
        unit_copies_kernel, "units", (centroids,), (array((far_size, local_count, width), bf16),), 4, 0
    )
    part = exchange(copies, far)
    copies = call(
        copies_kernel,
        "copies",
        (part, matched),
        (array((near_size,) + part.shape, bf16),),
        4,
        0,
        hbm_in=(1,),
    )
    group_centroids = exchange(copies, near).reshape(columns, width)

    product = 2 * row_count * columns
    row_parts = array((cent_size, row_count // LANES, LANES), f32)
    column_parts = array((x_size, columns // LANES, LANES), f32)
    column_sums = array((z_size, columns // LANES, LANES), f32)
    similarity, parts = call(
        similarity_kernel,
        "similarity",
        (unit_x, group_centroids, matched),
        (match_like, row_parts),
        16,
        product * width,
    )
    parts = exchange(parts, ("y", "core"))
    for sweep in range(SWEEPS):
        parts = call(column_kernel, "columns", (parts, similarity), (column_parts,), 8, product * 16)
        parts = call(sum_copies_kernel, "across", (exchange(parts, "x"),), (column_sums,), 2, 0)
        parts = call(
            functools.partial(row_kernel, desired_load),
            "rows",
            (exchange(parts, along_z), similarity),
            (row_parts,),
            8,
            product * 16,
        )
        parts = exchange(parts, ("y", "core"))
    chunk_rows = width // LANES * local_count
    sums = call(
        functools.partial(numerator_kernel, local_count),
        "numerator",
        (parts, similarity, embeddings),
        (array((near_size, far_size * chunk_rows + 16, LANES), bf16),),
        16,
        product * width,
        scratch=[pltpu.VMEM((row_count, columns), bf16)],
    )
    sums = call(
        functools.partial(hand_on_kernel, local_count),
        "hand_on",
        (exchange(sums, near),),
        (array((far_size, chunk_rows + 8, LANES), bf16),),
        8,
        0,
    )
    return call(
        update_kernel,
        "update",
        (exchange(sums, far), centroids),
        (array(centroids.shape, f32),),
        4,
        0,
    )


def solution(mesh):
    fine = Mesh(mesh.devices.reshape(4, 8, 2, 4, 2), ("x", "zh", "zl", "y", "core"))
    rows, held = P(("x", "zh", "zl"), None), P(("x", "zh", "zl", "y", "core"), None)
    return jax.shard_map(
        per_device,
        mesh=fine,
        in_specs=(rows, rows, held, P()),
        out_specs=held,
        check_vma=False,
    )
```
